128 devices in a mesh: by: 4 (over y_hi, core), bz: 32 (over x, z, y_lo).
Axes of the slice: x: 4, y: 4 (y_hi: 2, y_lo: 2; y = y_hi * 2 + y_lo), z: 4, core: 2. Of those that a mesh axis runs over, the one named last changes fastest.
Arguments:
- fields: float32 [8, 64, 1024, 512], P(None, 'by', 'bz'), may hold values from -400 to 400
- conductance: float32 [64, 1024, 512], P('by', 'bz'), may hold values from 0.05 to 1
Outputs:
- basis: float32 [8, 64, 1024, 512], P(None, 'by', 'bz')
- factor: float32 [512, 512], replicated
The draws below stay inside these ranges and needn't reach their ends.
All inputs are finite; a program needn't handle non-finite values.
Results may differ from the reference program's by a relative error of at most 0.0003.
Values sent between devices are 32-bit elements; how exact they have to be, the bound alone decides.
No kernel may reach another device: no remote copies, remote signals or barrier semaphores. Data moves between devices by JAX's collectives and lax.ppermute only.
A program may use at most 320 MiB of HBM per device.

```python
import math
import jax
import jax.numpy as jnp
from jax import lax

X = 512
F = 8
NY = 64
NZ = 1024


def draw_fields(key, part):
    key = jax.random.fold_in(key, 11)
    key_base, key_rows, key_cols = jax.random.split(key, 3)
    row_scale = jnp.exp(jax.random.uniform(key_rows, (F, NY, NZ, 1), minval=0.0, maxval=math.log(10.0)))
    col_scale = jnp.exp(jax.random.uniform(key_cols, (1, 1, 1, X), minval=0.0, maxval=math.log(10.0)))
    value = jnp.clip(jax.random.normal(key_base, (F, NY, NZ, X)), -4.0, 4.0) * row_scale * col_scale
    return value.astype(jnp.float32)


def level_of(stream_key, dims, cuts, low, high):
    loudness, own = 1.0, jax.random.fold_in(stream_key, 6)
    for dim, blocks in cuts:
        draws = jnp.exp(jax.random.uniform(jax.random.fold_in(own, dim), (blocks,), jnp.float32, low / len(cuts), high / len(cuts)))
        loudness = loudness * jnp.repeat(draws, dims[dim] // blocks).reshape([-1 if axis == dim else 1 for axis in range(len(dims))])
    return loudness


def setup_inputs(seed: int = 0) -> dict:
    seeds = jax.random.split(jax.random.key(seed), 3)
    return {
        "fields": draw_fields(jax.random.fold_in(seeds[2], 71), 0),
        "conductance": jnp.clip(jnp.exp(math.log(1.0) - 2.9957323 * jax.random.uniform(seeds[1], (NY, NZ, X), jnp.float32) ** level_of(seeds[1], (NY, NZ, X), ((0, 4), (1, 32)), -0.2, 0.2)), 0.05, 1.0),
    }


def relax(field, cond):
    padded = jnp.pad(field, 1)
    padk = jnp.pad(cond, 1)
    centre = field
    total = jnp.zeros_like(field)
    shapes = [(2, 1, 1), (0, 1, 1), (1, 2, 1), (1, 0, 1), (1, 1, 2), (1, 1, 0)]
    for start in shapes:
        nb = lax.slice(padded, start, (start[0] + field.shape[0], start[1] + field.shape[1], start[2] + field.shape[2]))
        kn = lax.slice(padk, start, (start[0] + field.shape[0], start[1] + field.shape[1], start[2] + field.shape[2]))
        total = total + jnp.sqrt(cond * kn) * (nb - centre)
    return centre + 0.125 * total

def reference(fields, conductance):

    def per_field(gram, field):
        once = relax(field, conductance)
        twice = relax(once, conductance)
        rows = twice.reshape(-1, twice.shape[-1])
        gram = gram + lax.dot_general(rows.astype(jnp.float32), rows.astype(jnp.float32), (((0,), (0,)), ((), ())), precision=lax.Precision.HIGHEST, preferred_element_type=jnp.float32)
        return (gram, twice)
    gram, relaxed = lax.scan(per_field, jnp.zeros((X, X), jnp.float32), fields)
    gram = gram / jnp.float32(F * NY * NZ)
    factor = jnp.linalg.cholesky(gram).T
    inverse = jax.scipy.linalg.solve_triangular(factor, jnp.eye(X, dtype=jnp.float32), lower=False)

    def project(field):
        rows = field.reshape(-1, X)
        return jnp.dot(rows.astype(jnp.float32), inverse.astype(jnp.float32), precision=lax.Precision.HIGHEST, preferred_element_type=jnp.float32).reshape(field.shape)
    basis = lax.map(project, relaxed)
    return (basis, factor)
```

```python
import jax
import jax.numpy as jnp
from jax import lax
from jax.experimental import pallas as pl
from jax.experimental.pallas import tpu as pltpu
from jax.sharding import Mesh, PartitionSpec as P

HI = lax.Precision.HIGHEST
BLK = 128
PAN = 16
Y_AXES = ("yh", "yl")

def with_halo(cells, sides, width):
    for axis, dim in sides:
        count = axis_count(axis)
        ends = count - 1
        head = lax.slice_in_dim(cells, 0, width, axis=dim)
        tail = lax.slice_in_dim(cells, cells.shape[dim] - width, cells.shape[dim], axis=dim)
        cells = jnp.concatenate(
            [
                lax.ppermute(tail, axis, [(i, (i + 1) % count) for i in range(ends)]),
                cells,
                lax.ppermute(head, axis, [((i + 1) % count, i) for i in range(ends)]),
            ],
            axis=dim,
        )
    return cells


def relax_inner(field_ext, cond_ext):
    centre = field_ext[:, 1:-1, 1:-1, :]
    kc = cond_ext[1:-1, 1:-1, :]
    total = jnp.zeros_like(centre)
    for nb, kn in (
        (field_ext[:, 2:, 1:-1, :], cond_ext[2:, 1:-1, :]),
        (field_ext[:, :-2, 1:-1, :], cond_ext[:-2, 1:-1, :]),
        (field_ext[:, 1:-1, 2:, :], cond_ext[1:-1, 2:, :]),
        (field_ext[:, 1:-1, :-2, :], cond_ext[1:-1, :-2, :]),
    ):
        total = total + jnp.sqrt(kc * kn)[None] * (nb - centre)
    padded = jnp.pad(centre, ((0, 0), (0, 0), (0, 0), (1, 1)))
    padk = jnp.pad(kc, ((0, 0), (0, 0), (1, 1)))
    total = total + jnp.sqrt(kc * padk[:, :, 2:])[None] * (padded[:, :, :, 2:] - centre)
    total = total + jnp.sqrt(kc * padk[:, :, :-2])[None] * (padded[:, :, :, :-2] - centre)
    return centre + 0.125 * total


def matmul_high(left, right):
    return jnp.dot(left, right, precision=lax.Precision.HIGHEST, preferred_element_type=jnp.float32)


def axis_count(axes):
    count = 1
    for axis in axes:
        count *= lax.axis_size(axis)
    return count


def shifted(piece, axes, count, distance):
    return lax.ppermute(piece, axes, [(i, (i + distance) % count) for i in range(count)])


def scatter_sum(pieces, axes, count):
    me = lax.axis_index(axes)
    own = lax.dynamic_index_in_dim(pieces, me, 0, keepdims=False)
    for d in range(1, count):
        send = lax.dynamic_index_in_dim(pieces, (me + d) % count, 0, keepdims=False)
        own = own + shifted(send, axes, count, d)
    return own


def gather(piece, axes, count):
    me = lax.axis_index(axes)
    out = jnp.zeros((count,) + piece.shape, piece.dtype)
    for d in range(count):
        part = piece if d == 0 else shifted(piece, axes, count, d)
        out = lax.dynamic_update_index_in_dim(out, part, (me - d) % count, 0)
    return out


def exchange_sum(piece, axes, count):
    total = piece
    for d in range(1, count):
        total = total + shifted(piece, axes, count, d)
    return total


def sum_over_devices(blocks):
    shape = blocks.shape
    x = blocks.reshape(2, 4, -1, shape[-1])
    x = scatter_sum(x, ("c",), 2)
    x = scatter_sum(x, Y_AXES, 4)
    x = exchange_sum(x, ("z",), 4)
    x = exchange_sum(x, ("x",), 4)
    x = gather(x, Y_AXES, 4)
    x = gather(x, ("c",), 2)
    return x.reshape(shape)


def rows_of(x,k):
    return jnp.broadcast_to(x[k:k+1,:],(8,x.shape[1]))

def diag_factor(work, PAN=PAN):
    nt=PAN//8
    iota=lax.broadcasted_iota(jnp.int32,(8,128),0)
    for p in range(BLK//PAN):
        j=p*PAN
        left=[work[j+8*t:j+8*t+8,0:128] for t in range(nt)]
        right=[work[j+8*t:j+8*t+8,128:256] for t in range(nt)]
        cols=[[jnp.broadcast_to(left[t][:,j+k:j+k+1],(8,128)) for t in range(nt)] for k in range(PAN)]
        scale=[jnp.zeros((8,128),jnp.float32) for _ in range(nt)]
        for k in range(PAN):
            t0,s0=k//8,k%8
            d=rows_of(cols[k][t0],s0)
            inv=1.0/d
            scale[t0]=jnp.where(iota==s0,lax.rsqrt(d),scale[t0])
            coef=[None]*nt
            for t in range(t0,nt):
                c=cols[k][t]*inv
                if t==t0: c=jnp.where(iota>s0,c,0.0)
                coef[t]=c
            for m in range(k+1,PAN):
                b=rows_of(cols[m][t0],s0)
                for t in range(t0,nt):
                    cols[m][t]=cols[m][t]-coef[t]*b
            for arr in (left,right):
                b=rows_of(arr[t0],s0)
                for t in range(t0,nt):
                    arr[t]=arr[t]-coef[t]*b
        left=[l*s for l,s in zip(left,scale)]
        right=[l*s for l,s in zip(right,scale)]
        for t in range(nt):
            work[j+8*t:j+8*t+8,0:128]=left[t]
            work[j+8*t:j+8*t+8,128:256]=right[t]
        if j+PAN<BLK:
            L=jnp.concatenate(left,0)
            R=jnp.concatenate([L,jnp.concatenate(right,0)],1)
            up=lax.dot_general(L,R,(((0,),(0,)),((),())),precision=HI,preferred_element_type=jnp.float32)
            work[j+PAN:BLK,:]=work[j+PAN:BLK,:]-up[j+PAN:BLK,:]

def factor_kernel(g_ref,fac_ref,n_ref,work):
    n=n_ref.shape[0]
    cnt=n//BLK
    t=0
    for i in range(cnt):
        for j in range(i,cnt):
            n_ref[i*BLK:(i+1)*BLK,j*BLK:(j+1)*BLK]=g_ref[t]
            t+=1
    r=lax.broadcasted_iota(jnp.int32,(BLK,BLK),0)
    c=lax.broadcasted_iota(jnp.int32,(BLK,BLK),1)
    for k in range(cnt):
        lo,hi=k*BLK,(k+1)*BLK
        work[:,0:128]=n_ref[lo:hi,lo:hi]
        work[:,128:256]=jnp.where(r==c,1.0,0.0)
        diag_factor(work)
        rkk=jnp.where(r<=c,work[:,0:128],0.0)
        m=jnp.where(r>=c,work[:,128:256],0.0)
        fac_ref[lo:hi,lo:hi]=rkk
        if lo>0:
            fac_ref[lo:hi,0:lo]=jnp.zeros((BLK,lo),jnp.float32)
            n_ref[lo:hi,0:lo]=jnp.dot(m,n_ref[lo:hi,0:lo],precision=HI,preferred_element_type=jnp.float32)
        n_ref[lo:hi,lo:hi]=m
        if hi<n:
            rk=jnp.dot(m,n_ref[lo:hi,hi:n],precision=HI,preferred_element_type=jnp.float32)
            fac_ref[lo:hi,hi:n]=rk
            n_ref[lo:hi,hi:n]=jnp.zeros((BLK,n-hi),jnp.float32)
            upn=lax.dot_general(rk,n_ref[lo:hi,0:hi],(((0,),(0,)),((),())),precision=HI,preferred_element_type=jnp.float32)
            if lo>0: n_ref[hi:n,0:lo]=n_ref[hi:n,0:lo]-upn[:,0:lo]
            n_ref[hi:n,lo:hi]=-upn[:,lo:hi]
            upw=lax.dot_general(rk,rk,(((0,),(0,)),((),())),precision=HI,preferred_element_type=jnp.float32)
            for i in range(k+1,cnt):
                a=i*BLK
                n_ref[a:a+BLK,a:n]=n_ref[a:a+BLK,a:n]-upw[a-hi:a-hi+BLK,a-hi:]


def factor_and_inverse(blocks, n):
    square = jax.ShapeDtypeStruct((n, n), jnp.float32)
    whole = pl.BlockSpec(memory_space=pltpu.VMEM)
    return pl.pallas_call(
        factor_kernel,
        out_shape=(square, square),
        in_specs=[whole],
        out_specs=(whole, whole),
        scratch_shapes=[pltpu.VMEM((BLK, 2 * BLK), jnp.float32)],
        compiler_params=pltpu.CompilerParams(vmem_limit_bytes=32 * 2**20),
    )(blocks)

BY = ("yh", "c")
BZ = ("x", "z", "yl")

def on_device(fields, conductance):
    nfield = fields.shape[0]
    width = fields.shape[3]
    stacked = jnp.concatenate([fields, conductance[None]], axis=0)
    extended = with_halo(stacked, ((BY, 1), (BZ, 2)), 1)
    once = relax_inner(extended[:nfield], extended[nfield])
    again = with_halo(once, ((BY, 1), (BZ, 2)), 1)
    relaxed = relax_inner(again, extended[nfield])
    total_rows = nfield * fields.shape[1] * axis_count(BY) * fields.shape[2] * axis_count(BZ)
    rows = relaxed.reshape(-1, width)
    local_gram = lax.dot_general(
        rows,
        rows,
        (((0,), (0,)), ((), ())),
        precision=lax.Precision.HIGHEST,
        preferred_element_type=jnp.float32,
    )
    local_gram = local_gram / jnp.float32(total_rows)
    count = width // BLK
    blocks = jnp.stack(
        [
            local_gram[i * BLK : (i + 1) * BLK, j * BLK : (j + 1) * BLK]
            for i in range(count)
            for j in range(i, count)
        ]
    )
    factor, inverse_t = factor_and_inverse(sum_over_devices(blocks), width)
    basis = lax.dot_general(
        rows, inverse_t, (((1,), (1,)), ((), ())), precision=HI, preferred_element_type=jnp.float32
    )
    return (basis.reshape(relaxed.shape), factor)


def solution(mesh):
    fine = Mesh(mesh.devices.reshape(2, 2, 4, 4, 2), ("yh", "c", "x", "z", "yl"))
    return jax.shard_map(
        on_device,
        mesh=fine,
        in_specs=(P(None, BY, BZ, None), P(BY, BZ, None)),
        out_specs=(P(None, BY, BZ, None), P()),
        check_vma=False,
    )
```

```python
import jax
import jax.numpy as jnp
from jax import lax
from jax.experimental import pallas as pl
from jax.experimental.pallas import tpu as pltpu
from jax.sharding import Mesh, PartitionSpec as P

HI = lax.Precision.HIGHEST
BLK = 128
PAN = 16
Y_AXES = ("yh", "yl")

def shifted(piece, axes, count, distance):
    return lax.ppermute(piece, axes, [(i, (i + distance) % count) for i in range(count)])


def scatter_sum(pieces, axes, count):
    me = lax.axis_index(axes)
    own = lax.dynamic_index_in_dim(pieces, me, 0, keepdims=False)
    for d in range(1, count):
        send = lax.dynamic_index_in_dim(pieces, (me + d) % count, 0, keepdims=False)
        own = own + shifted(send, axes, count, d)
    return own


def gather(piece, axes, count):
    me = lax.axis_index(axes)
    out = jnp.zeros((count,) + piece.shape, piece.dtype)
    for d in range(count):
        part = piece if d == 0 else shifted(piece, axes, count, d)
        out = lax.dynamic_update_index_in_dim(out, part, (me - d) % count, 0)
    return out


def exchange_sum(piece, axes, count):
    total = piece
    for d in range(1, count):
        total = total + shifted(piece, axes, count, d)
    return total


def sum_over_devices(blocks):
    shape = blocks.shape
    x = blocks.reshape(2, 4, -1, shape[-1])
    x = scatter_sum(x, ("c",), 2)
    x = scatter_sum(x, Y_AXES, 4)
    x = exchange_sum(x, ("z",), 4)
    x = exchange_sum(x, ("x",), 4)
    x = gather(x, Y_AXES, 4)
    x = gather(x, ("c",), 2)
    return x.reshape(shape)


def rows_of(x,k):
    return jnp.broadcast_to(x[k:k+1,:],(8,x.shape[1]))

def diag_factor(work, PAN=PAN):
    nt=PAN//8
    iota=lax.broadcasted_iota(jnp.int32,(8,128),0)
    for p in range(BLK//PAN):
        j=p*PAN
        left=[work[j+8*t:j+8*t+8,0:128] for t in range(nt)]
        right=[work[j+8*t:j+8*t+8,128:256] for t in range(nt)]
        cols=[[jnp.broadcast_to(left[t][:,j+k:j+k+1],(8,128)) for t in range(nt)] for k in range(PAN)]
        scale=[jnp.zeros((8,128),jnp.float32) for _ in range(nt)]
        for k in range(PAN):
            t0,s0=k//8,k%8
            d=rows_of(cols[k][t0],s0)
            inv=1.0/d
            scale[t0]=jnp.where(iota==s0,lax.rsqrt(d),scale[t0])
            coef=[None]*nt
            for t in range(t0,nt):
                c=cols[k][t]*inv
                if t==t0: c=jnp.where(iota>s0,c,0.0)
                coef[t]=c
            for m in range(k+1,PAN):
                b=rows_of(cols[m][t0],s0)
                for t in range(t0,nt):
                    cols[m][t]=cols[m][t]-coef[t]*b
            for arr in (left,right):
                b=rows_of(arr[t0],s0)
                for t in range(t0,nt):
                    arr[t]=arr[t]-coef[t]*b
        left=[l*s for l,s in zip(left,scale)]
        right=[l*s for l,s in zip(right,scale)]
        for t in range(nt):
            work[j+8*t:j+8*t+8,0:128]=left[t]
            work[j+8*t:j+8*t+8,128:256]=right[t]
        if j+PAN<BLK:
            L=jnp.concatenate(left,0)
            R=jnp.concatenate([L,jnp.concatenate(right,0)],1)
            up=lax.dot_general(L,R,(((0,),(0,)),((),())),precision=HI,preferred_element_type=jnp.float32)
            work[j+PAN:BLK,:]=work[j+PAN:BLK,:]-up[j+PAN:BLK,:]

def factor_kernel(g_ref,fac_ref,n_ref,work):
    n=n_ref.shape[0]
    cnt=n//BLK
    t=0
    for i in range(cnt):
        for j in range(i,cnt):
            n_ref[i*BLK:(i+1)*BLK,j*BLK:(j+1)*BLK]=g_ref[t]
            t+=1
    r=lax.broadcasted_iota(jnp.int32,(BLK,BLK),0)
    c=lax.broadcasted_iota(jnp.int32,(BLK,BLK),1)
    for k in range(cnt):
        lo,hi=k*BLK,(k+1)*BLK
        work[:,0:128]=n_ref[lo:hi,lo:hi]
        work[:,128:256]=jnp.where(r==c,1.0,0.0)
        diag_factor(work)
        rkk=jnp.where(r<=c,work[:,0:128],0.0)
        m=jnp.where(r>=c,work[:,128:256],0.0)
        fac_ref[lo:hi,lo:hi]=rkk
        if lo>0:
            fac_ref[lo:hi,0:lo]=jnp.zeros((BLK,lo),jnp.float32)
            n_ref[lo:hi,0:lo]=jnp.dot(m,n_ref[lo:hi,0:lo],precision=HI,preferred_element_type=jnp.float32)
        n_ref[lo:hi,lo:hi]=m
        if hi<n:
            rk=jnp.dot(m,n_ref[lo:hi,hi:n],precision=HI,preferred_element_type=jnp.float32)
            fac_ref[lo:hi,hi:n]=rk
            n_ref[lo:hi,hi:n]=jnp.zeros((BLK,n-hi),jnp.float32)
            upn=lax.dot_general(rk,n_ref[lo:hi,0:hi],(((0,),(0,)),((),())),precision=HI,preferred_element_type=jnp.float32)
            if lo>0: n_ref[hi:n,0:lo]=n_ref[hi:n,0:lo]-upn[:,0:lo]
            n_ref[hi:n,lo:hi]=-upn[:,lo:hi]
            upw=lax.dot_general(rk,rk,(((0,),(0,)),((),())),precision=HI,preferred_element_type=jnp.float32)
            for i in range(k+1,cnt):
                a=i*BLK
                n_ref[a:a+BLK,a:n]=n_ref[a:a+BLK,a:n]-upw[a-hi:a-hi+BLK,a-hi:]


def factor_and_inverse(blocks, n):
    square = jax.ShapeDtypeStruct((n, n), jnp.float32)
    whole = pl.BlockSpec(memory_space=pltpu.VMEM)
    return pl.pallas_call(
        factor_kernel,
        out_shape=(square, square),
        in_specs=[whole],
        out_specs=(whole, whole),
        scratch_shapes=[pltpu.VMEM((BLK, 2 * BLK), jnp.float32)],
        compiler_params=pltpu.CompilerParams(vmem_limit_bytes=32 * 2**20),
    )(blocks)


def ahead(a, axis):
    return pltpu.roll(a, a.shape[axis] - 1, axis)


def behind(a, axis):
    return pltpu.roll(a, 1, axis)


def link(a, b):
    return 0.125 * jnp.sqrt(a * b)


def link_along(k, axis):
    n = k.shape[axis]
    at = lax.broadcasted_iota(jnp.int32, k.shape, axis)
    return jnp.where(at < n - 1, link(k, ahead(k, axis)), 0.0)


def flow_along(u, w, axis):
    flux = w * (ahead(u, axis) - u)
    return flux - behind(flux, axis)


def add_first_row(a, row):
    top = a[0:8]
    at = lax.broadcasted_iota(jnp.int32, top.shape, 0)
    top = top + jnp.where(at == 0, jnp.broadcast_to(row, top.shape), 0.0)
    return jnp.concatenate([top, a[8:]], 0)


def add_last_row(a, row):
    n = a.shape[0]
    end = a[n - 8 :]
    at = lax.broadcasted_iota(jnp.int32, end.shape, 0)
    end = end + jnp.where(at == 7, jnp.broadcast_to(row, end.shape), 0.0)
    return jnp.concatenate([a[: n - 8], end], 0)


def relax_slabs(u, wx, wy, wz, emit):
    count = wx.shape[0]
    below = None
    for y in range(count):
        c = u(y)
        t = flow_along(c, wx[y], 1) + flow_along(c, wz[y], 0)
        if below is not None:
            t = t - below
        if y + 1 < count:
            below = wy[y] * (u(y + 1) - c)
            t = t + below
        emit(y, c, t)


def own_kernel(f_ref, k_ref, p_ref, wx, wy, wz, pzlo, pzhi):
    count, nz, _ = k_ref.shape

    @pl.when(pl.program_id(0) == 0)
    def _():
        for y in range(count):
            k = k_ref[y]
            wx[y] = link_along(k, 1)
            wz[y] = link_along(k, 0)
            wy[y] = link(k, k_ref[y + 1]) if y + 1 < count else jnp.zeros_like(k)

    def emit(y, c, t):
        r = c + t
        p_ref[0, y] = r
        pzlo[0, y : y + 1] = r[0:1]
        pzhi[0, y : y + 1] = r[nz - 1 : nz]

    relax_slabs(lambda y: f_ref[0, y], wx, wy, wz, emit)


def limit(mib):
    return pltpu.CompilerParams(vmem_limit_bytes=mib * 2**20)


def own_relax(fields, conductance):
    nf, ny, nz, nx = fields.shape
    block = pl.BlockSpec((1, ny, nz, nx), lambda f: (f, 0, 0, 0))
    whole = pl.BlockSpec((ny, nz, nx), lambda f: (0, 0, 0))
    zface = pl.BlockSpec((1, ny, nx), lambda f: (f, 0, 0))
    w = jax.ShapeDtypeStruct((ny, nz, nx), jnp.float32)
    zf = jax.ShapeDtypeStruct((nf, ny, nx), jnp.float32)
    return pl.pallas_call(
        own_kernel,
        grid=(nf,),
        in_specs=[block, whole],
        out_specs=(block, whole, whole, whole, zface, zface),
        out_shape=(jax.ShapeDtypeStruct(fields.shape, jnp.float32), w, w, w, zf, zf),
        compiler_params=limit(18),
    )(fields, conductance)


def face_kernel(
    p0, p1, pzlo, pzhi, ylo, yhi, zlo, zhi, yu, yd, zl, zr,
    oylo, oyhi, ozlo, ozhi, lyu, lyd, lzl, lzr,
):
    nf, _, nz, _ = p0.shape
    ny = pzlo.shape[1]
    lyu[...] = link(ylo[nf, 0], yu[nf, 0])
    lyd[...] = link(yhi[nf, 0], yd[nf, 0])
    lzl[...] = link(zlo[nf], zl[nf])
    lzr[...] = link(zhi[nf], zr[nf])
    for f in range(nf):
        up = lyu[...] * (yu[f, 0] - ylo[f, 0])
        down = lyd[...] * (yd[f, 0] - yhi[f, 0])
        left = lzl[...] * (zl[f] - zlo[f])
        right = lzr[...] * (zr[f] - zhi[f])

        def both(a, first, last):
            return add_last_row(add_first_row(a, first), last)

        oylo[f, 0] = both(p0[f, 0] + up, left[0:1], right[0:1])
        oyhi[f, 0] = both(p1[f, 0] + down, left[ny - 1 : ny], right[ny - 1 : ny])
        ozlo[f] = both(pzlo[f] + left, up[0:1], down[0:1])
        ozhi[f] = both(pzhi[f] + right, up[nz - 1 : nz], down[nz - 1 : nz])


def face_relax(p, pzlo, pzhi, ylo, yhi, zlo, zhi, yu, yd, zl, zr):
    nf, ny, nz, nx = p.shape
    full = lambda a: pl.BlockSpec(a.shape, lambda i: (0,) * len(a.shape))
    slab = lambda y: pl.BlockSpec((nf, 1, nz, nx), lambda i: (0, y, 0, 0))
    rest = (pzlo, pzhi, ylo, yhi, zlo, zhi, yu, yd, zl, zr)
    ys = jax.ShapeDtypeStruct((nf, 1, nz, nx), jnp.float32)
    zs = jax.ShapeDtypeStruct((nf, ny, nx), jnp.float32)
    ly = jax.ShapeDtypeStruct((nz, nx), jnp.float32)
    lz = jax.ShapeDtypeStruct((ny, nx), jnp.float32)
    outs = (ys, ys, zs, zs, ly, ly, lz, lz)
    return pl.pallas_call(
        face_kernel,
        grid=(1,),
        in_specs=[slab(0), slab(ny - 1)] + [full(a) for a in rest],
        out_specs=tuple(full(a) for a in outs),
        out_shape=outs,
        compiler_params=limit(20),
    )(p, p, *rest)


def again_kernel(p_ref, wx, wy, wz, oylo, oyhi, ozlo, ozhi, t_ref, once):
    ny, nz, _ = wx.shape
    for y in range(ny):
        if y == 0:
            once[y] = oylo[0, 0]
        elif y == ny - 1:
            once[y] = oyhi[0, 0]
        else:
            once[y] = p_ref[0, y]
            once[y, 0:1] = ozlo[0, y : y + 1]
            once[y, nz - 1 : nz] = ozhi[0, y : y + 1]

    def emit(y, c, t):
        t_ref[0, y] = c + t

    relax_slabs(lambda y: once[y], wx, wy, wz, emit)


def specs(nf, ny, nz, nx):
    block = pl.BlockSpec((1, ny, nz, nx), lambda f: (f, 0, 0, 0))
    yface = pl.BlockSpec((1, 1, nz, nx), lambda f: (f, 0, 0, 0))
    zface = pl.BlockSpec((1, ny, nx), lambda f: (f, 0, 0))
    return block, yface, zface


def again_relax(p, wx, wy, wz, *faces):
    nf, ny, nz, nx = p.shape
    block, yface, zface = specs(*p.shape)
    whole = pl.BlockSpec((ny, nz, nx), lambda f: (0, 0, 0))
    return pl.pallas_call(
        again_kernel,
        grid=(nf,),
        in_specs=[block, whole, whole, whole, yface, yface, zface, zface],
        out_specs=block,
        out_shape=jax.ShapeDtypeStruct(p.shape, jnp.float32),
        scratch_shapes=[pltpu.VMEM((ny, nz, nx), jnp.float32)],
        compiler_params=limit(18),
    )(p, wx, wy, wz, *faces)


def edge_kernel(
    t_ref, oylo, oyhi, ozlo, ozhi, yu, yd, zl, zr, lyu, lyd, lzl, lzr,
    r_ref, g_ref, high, low,
):
    f = pl.program_id(0)
    _, ny, nz, nx = t_ref.shape
    left = lzl[...] * (zl[0] - ozlo[0])
    right = lzr[...] * (zr[0] - ozhi[0])
    for y in range(ny):
        r = t_ref[0, y]
        if y == 0:
            r = r + lyu[...] * (yu[0, 0] - oylo[0, 0])
        if y == ny - 1:
            r = r + lyd[...] * (yd[0, 0] - oyhi[0, 0])
        r = add_first_row(r, left[y : y + 1])
        r = add_last_row(r, right[y : y + 1])
        r_ref[0, y] = r
        h = r.astype(jnp.bfloat16)
        at = pl.ds(pl.multiple_of(f * (ny * nz) + y * nz, nz), nz)
        high[at] = h
        low[at] = (r - h.astype(jnp.float32)).astype(jnp.bfloat16)

    def cross(a, b):
        return lax.dot_general(a, b, (((0,), (0,)), ((), ())), preferred_element_type=jnp.float32)

    @pl.when(f == pl.num_programs(0) - 1)
    def _():
        half = nx // 2
        part = (slice(0, half), slice(half, nx))
        acc_hh, acc_hl = [], []
        for i in range(3):
            a, b = part[i // 2], part[(i + 1) // 2]
            acc_hh.append(cross(high[:, a], high[:, b]) + cross(low[:, a], low[:, b]))
        for i in range(4):
            acc_hl.append(cross(high[:, part[i // 2]], low[:, part[i % 2]]))
        per = half // BLK

        def inner_block(i, j):
            return slice(i % per * BLK, (i % per + 1) * BLK), slice(j % per * BLK, (j % per + 1) * BLK)

        t = 0
        for i in range(2 * per):
            for j in range(i, 2 * per):
                p, q = i // per, j // per
                a, b = inner_block(i, j)
                g_ref[t] = acc_hh[p + q][a, b] + acc_hl[2 * p + q][a, b] + acc_hl[2 * q + p][b, a].T
                t += 1


def edge_relax(t, faces, halos, links):
    nf, ny, nz, nx = t.shape
    block, yface, zface = specs(*t.shape)
    ly = pl.BlockSpec((nz, nx), lambda f: (0, 0))
    lz = pl.BlockSpec((ny, nx), lambda f: (0, 0))
    cnt = nx // BLK
    nb = cnt * (cnt + 1) // 2
    return pl.pallas_call(
        edge_kernel,
        grid=(nf,),
        in_specs=[block] + [yface, yface, zface, zface] * 2 + [ly, ly, lz, lz],
        out_specs=(block, pl.BlockSpec((nb, BLK, BLK), lambda f: (0, 0, 0))),
        out_shape=(
            jax.ShapeDtypeStruct(t.shape, jnp.float32),
            jax.ShapeDtypeStruct((nb, BLK, BLK), jnp.float32),
        ),
        scratch_shapes=[pltpu.VMEM((nf * ny * nz, nx), jnp.bfloat16)] * 2,
        compiler_params=limit(24),
    )(t, *faces, *halos, *links)


def basis_kernel(r_ref, n_ref, o_ref, high, low):
    @pl.when(pl.program_id(0) == 0)
    def _():
        n = n_ref[...]
        h = n.astype(jnp.bfloat16)
        high[...] = h
        low[...] = (n - h.astype(jnp.float32)).astype(jnp.bfloat16)

    r = r_ref[...]
    a = r.astype(jnp.bfloat16)
    b = (r - a.astype(jnp.float32)).astype(jnp.bfloat16)
    width = r.shape[1]
    step = 256
    for lo in range(0, width, step):
        hi = lo + step

        def times(x, m):
            return lax.dot_general(
                x[:, 0:hi], m[lo:hi, 0:hi], (((1,), (1,)), ((), ())), preferred_element_type=jnp.float32
            )

        o_ref[:, lo:hi] = times(a, high) + (times(a, low) + times(b, high))


def basis_of(rows, inverse_t, chunk=512):
    m, nx = rows.shape
    block = pl.BlockSpec((chunk, nx), lambda i: (i, 0))
    return pl.pallas_call(
        basis_kernel,
        grid=(m // chunk,),
        in_specs=[block, pl.BlockSpec((nx, nx), lambda i: (0, 0))],
        out_specs=block,
        out_shape=jax.ShapeDtypeStruct((m, nx), jnp.float32),
        scratch_shapes=[pltpu.VMEM((nx, nx), jnp.bfloat16)] * 2,
        compiler_params=pltpu.CompilerParams(vmem_limit_bytes=14 * 2**20),
    )(rows, inverse_t)

BY = ("yh", "c")
BZ = ("x", "z", "yl")


def axis_count(axes):
    count = 1
    for axis in axes:
        count *= lax.axis_size(axis)
    return count


def from_next(piece, axes, step):
    n = axis_count(axes)
    return lax.ppermute(piece, axes, [(i + step, i) for i in range(n) if 0 <= i + step < n])


def on_device(fields, conductance):
    nfield, ny, nz, width = fields.shape

    def cells(ys, zs):
        return jnp.concatenate([fields[:, ys, zs], conductance[None, ys, zs]], axis=0)

    every = slice(None)
    ylo, yhi = cells(slice(0, 1), every), cells(slice(-1, None), every)
    zlo, zhi = cells(every, 0), cells(every, -1)

    def neighbours(ylo, yhi, zlo, zhi):
        return from_next(yhi, BY, -1), from_next(ylo, BY, 1), from_next(zhi, BZ, -1), from_next(zlo, BZ, 1)

    halo = neighbours(ylo, yhi, zlo, zhi)
    part, wx, wy, wz, pzlo, pzhi = own_relax(fields, conductance)
    out = face_relax(part, pzlo, pzhi, ylo, yhi, zlo, zhi, *halo)
    faces, links = out[:4], out[4:]
    halo = neighbours(*faces)
    twice = again_relax(part, wx, wy, wz, *faces)
    relaxed, blocks = edge_relax(twice, faces, halo, links)
    total_rows = nfield * ny * axis_count(BY) * nz * axis_count(BZ)
    blocks = sum_over_devices(blocks) / jnp.float32(total_rows)
    factor, inverse_t = factor_and_inverse(blocks, width)
    basis = basis_of(relaxed.reshape(-1, width), inverse_t)
    return (basis.reshape(relaxed.shape), factor)


def solution(mesh):
    fine = Mesh(mesh.devices.reshape(2, 2, 4, 4, 2), ("yh", "c", "x", "z", "yl"))
    return jax.shard_map(
        on_device,
        mesh=fine,
        in_specs=(P(None, BY, BZ, None), P(BY, BZ, None)),
        out_specs=(P(None, BY, BZ, None), P()),
        check_vma=False,
    )
```

```python
import jax
import jax.numpy as jnp
from jax import lax
from jax.experimental import pallas as pl
from jax.experimental.pallas import tpu as pltpu
from jax.sharding import Mesh, PartitionSpec as P

HI = lax.Precision.HIGHEST
BLK = 128
PAN = 32
Y_AXES = ("yh", "yl")

def shifted(piece, axes, count, distance):
    return lax.ppermute(piece, axes, [(i, (i + distance) % count) for i in range(count)])


def scatter_sum(pieces, axes, count):
    me = lax.axis_index(axes)
    own = lax.dynamic_index_in_dim(pieces, me, 0, keepdims=False)
    for d in range(1, count):
        send = lax.dynamic_index_in_dim(pieces, (me + d) % count, 0, keepdims=False)
        own = own + shifted(send, axes, count, d)
    return own


def gather(piece, axes, count):
    me = lax.axis_index(axes)
    out = jnp.zeros((count,) + piece.shape, piece.dtype)
    for d in range(count):
        part = piece if d == 0 else shifted(piece, axes, count, d)
        out = lax.dynamic_update_index_in_dim(out, part, (me - d) % count, 0)
    return out


def exchange_sum(piece, axes, count):
    total = piece
    for d in range(1, count):
        total = total + shifted(piece, axes, count, d)
    return total


def sum_over_devices(blocks):
    shape = blocks.shape
    x = blocks.reshape(2, 4, -1, shape[-1])
    x = scatter_sum(x, ("c",), 2)
    x = scatter_sum(x, Y_AXES, 4)
    x = exchange_sum(x, ("z",), 4)
    x = exchange_sum(x, ("x",), 4)
    x = gather(x, Y_AXES, 4)
    x = gather(x, ("c",), 2)
    return x.reshape(shape)


def rows_of(x,k):
    return jnp.broadcast_to(x[k:k+1,:],(8,x.shape[1]))

def diag_factor(work, PAN=PAN):
    nt=PAN//8
    iota=lax.broadcasted_iota(jnp.int32,(8,128),0)
    for p in range(BLK//PAN):
        j=p*PAN
        left=[work[j+8*t:j+8*t+8,0:128] for t in range(nt)]
        right=[work[j+8*t:j+8*t+8,128:256] for t in range(nt)]
        cols=[[jnp.broadcast_to(left[t][:,j+k:j+k+1],(8,128)) for t in range(nt)] for k in range(PAN)]
        scale=[jnp.zeros((8,128),jnp.float32) for _ in range(nt)]
        for k in range(PAN):
            t0,s0=k//8,k%8
            d=rows_of(cols[k][t0],s0)
            inv=1.0/d
            scale[t0]=jnp.where(iota==s0,lax.rsqrt(d),scale[t0])
            coef=[None]*nt
            for t in range(t0,nt):
                c=cols[k][t]*inv
                if t==t0: c=jnp.where(iota>s0,c,0.0)
                coef[t]=c
            for m in range(k+1,PAN):
                b=rows_of(cols[m][t0],s0)
                for t in range(t0,nt):
                    cols[m][t]=cols[m][t]-coef[t]*b
            for arr in (left,right):
                b=rows_of(arr[t0],s0)
                for t in range(t0,nt):
                    arr[t]=arr[t]-coef[t]*b
        left=[l*s for l,s in zip(left,scale)]
        right=[l*s for l,s in zip(right,scale)]
        for t in range(nt):
            work[j+8*t:j+8*t+8,0:128]=left[t]
            work[j+8*t:j+8*t+8,128:256]=right[t]
        if j+PAN<BLK:
            L=jnp.concatenate(left,0)
            R=jnp.concatenate([L,jnp.concatenate(right,0)],1)
            up=lax.dot_general(L,R,(((0,),(0,)),((),())),precision=HI,preferred_element_type=jnp.float32)
            work[j+PAN:BLK,:]=work[j+PAN:BLK,:]-up[j+PAN:BLK,:]

def factor_kernel(g_ref,fac_ref,n_ref,work):
    n=n_ref.shape[0]
    cnt=n//BLK
    t=0
    for i in range(cnt):
        for j in range(i,cnt):
            n_ref[i*BLK:(i+1)*BLK,j*BLK:(j+1)*BLK]=g_ref[t]
            t+=1
    r=lax.broadcasted_iota(jnp.int32,(BLK,BLK),0)
    c=lax.broadcasted_iota(jnp.int32,(BLK,BLK),1)
    for k in range(cnt):
        lo,hi=k*BLK,(k+1)*BLK
        work[:,0:128]=n_ref[lo:hi,lo:hi]
        work[:,128:256]=jnp.where(r==c,1.0,0.0)
        diag_factor(work)
        rkk=jnp.where(r<=c,work[:,0:128],0.0)
        m=jnp.where(r>=c,work[:,128:256],0.0)
        fac_ref[lo:hi,lo:hi]=rkk
        if lo>0:
            fac_ref[lo:hi,0:lo]=jnp.zeros((BLK,lo),jnp.float32)
            n_ref[lo:hi,0:lo]=jnp.dot(m,n_ref[lo:hi,0:lo],precision=HI,preferred_element_type=jnp.float32)
        n_ref[lo:hi,lo:hi]=m
        if hi<n:
            rk=jnp.dot(m,n_ref[lo:hi,hi:n],precision=HI,preferred_element_type=jnp.float32)
            fac_ref[lo:hi,hi:n]=rk
            n_ref[lo:hi,hi:n]=jnp.zeros((BLK,n-hi),jnp.float32)
            upn=lax.dot_general(rk,n_ref[lo:hi,0:hi],(((0,),(0,)),((),())),precision=HI,preferred_element_type=jnp.float32)
            if lo>0: n_ref[hi:n,0:lo]=n_ref[hi:n,0:lo]-upn[:,0:lo]
            n_ref[hi:n,lo:hi]=-upn[:,lo:hi]
            upw=lax.dot_general(rk,rk,(((0,),(0,)),((),())),precision=HI,preferred_element_type=jnp.float32)
            for i in range(k+1,cnt):
                a=i*BLK
                n_ref[a:a+BLK,a:n]=n_ref[a:a+BLK,a:n]-upw[a-hi:a-hi+BLK,a-hi:]


def factor_and_inverse(blocks, n):
    square = jax.ShapeDtypeStruct((n, n), jnp.float32)
    whole = pl.BlockSpec(memory_space=pltpu.VMEM)
    return pl.pallas_call(
        factor_kernel,
        out_shape=(square, square),
        in_specs=[whole],
        out_specs=(whole, whole),
        scratch_shapes=[pltpu.VMEM((BLK, 2 * BLK), jnp.float32)],
        compiler_params=pltpu.CompilerParams(vmem_limit_bytes=24 * 2**20),
    )(blocks)


def ahead(a, axis):
    return pltpu.roll(a, a.shape[axis] - 1, axis)


def behind(a, axis):
    return pltpu.roll(a, 1, axis)


def link(a, b):
    return 0.125 * jnp.sqrt(a * b)


def link_along(k, axis):
    n = k.shape[axis]
    at = lax.broadcasted_iota(jnp.int32, k.shape, axis)
    return jnp.where(at < n - 1, link(k, ahead(k, axis)), 0.0)


def flow_along(u, w, axis):
    flux = w * (ahead(u, axis) - u)
    return flux - behind(flux, axis)


def add_first_row(a, row):
    top = a[0:8]
    at = lax.broadcasted_iota(jnp.int32, top.shape, 0)
    top = top + jnp.where(at == 0, jnp.broadcast_to(row, top.shape), 0.0)
    return jnp.concatenate([top, a[8:]], 0)


def add_last_row(a, row):
    n = a.shape[0]
    end = a[n - 8 :]
    at = lax.broadcasted_iota(jnp.int32, end.shape, 0)
    end = end + jnp.where(at == 7, jnp.broadcast_to(row, end.shape), 0.0)
    return jnp.concatenate([a[: n - 8], end], 0)


def relax_slabs(u, wx, wy, wz, emit):
    count = wx.shape[0]
    below = None
    for y in range(count):
        c = u(y)
        t = flow_along(c, wx[y], 1) + flow_along(c, wz[y], 0)
        if below is not None:
            t = t - below
        if y + 1 < count:
            below = wy[y] * (u(y + 1) - c)
            t = t + below
        emit(y, c, t)


def own_kernel(f_ref, k_ref, p_ref, wx, wy, wz, pylo, pyhi, pzlo, pzhi):
    count, nz, _ = k_ref.shape

    @pl.when(pl.program_id(0) == 0)
    def _():
        for y in range(count):
            k = k_ref[y]
            wx[y] = link_along(k, 1)
            wz[y] = link_along(k, 0)
            wy[y] = link(k, k_ref[y + 1]) if y + 1 < count else jnp.zeros_like(k)

    def emit(y, c, t):
        r = c + t
        p_ref[0, y] = r
        if y == 0:
            pylo[0, 0] = r
        if y == count - 1:
            pyhi[0, 0] = r
        pzlo[0, y : y + 1] = r[0:1]
        pzhi[0, y : y + 1] = r[nz - 1 : nz]

    relax_slabs(lambda y: f_ref[0, y], wx, wy, wz, emit)


def far(x):
    return pltpu.with_memory_space_constraint(x, pltpu.HBM)


def limit(mib):
    return pltpu.CompilerParams(vmem_limit_bytes=mib * 2**20)


def own_relax(fields, conductance):
    nf, ny, nz, nx = fields.shape
    block = pl.BlockSpec((1, ny, nz, nx), lambda f: (f, 0, 0, 0))
    whole = pl.BlockSpec((ny, nz, nx), lambda f: (0, 0, 0))
    zface = pl.BlockSpec((1, ny, nx), lambda f: (f, 0, 0))
    w = pltpu.HBM((ny, nz, nx), jnp.float32)
    yf = jax.ShapeDtypeStruct((nf, 1, nz, nx), jnp.float32)
    yface = pl.BlockSpec((1, 1, nz, nx), lambda f: (f, 0, 0, 0))
    zf = jax.ShapeDtypeStruct((nf, ny, nx), jnp.float32)
    return pl.pallas_call(
        own_kernel,
        grid=(nf,),
        in_specs=[block, whole],
        out_specs=(block, whole, whole, whole, yface, yface, zface, zface),
        out_shape=(pltpu.HBM(fields.shape, jnp.float32), w, w, w, yf, yf, zf, zf),
        compiler_params=limit(24),
    )(far(fields), far(conductance))


def face_kernel(
    pylo, pyhi, pzlo, pzhi, ylo, yhi, zlo, zhi, yu, yd, zl, zr,
    oylo, oyhi, ozlo, ozhi, lyu, lyd, lzl, lzr,
):
    nf, _, nz, _ = pylo.shape
    ny = pzlo.shape[1]
    lyu[...] = link(ylo[nf, 0], yu[nf, 0])
    lyd[...] = link(yhi[nf, 0], yd[nf, 0])
    lzl[...] = link(zlo[nf], zl[nf])
    lzr[...] = link(zhi[nf], zr[nf])
    for f in range(nf):
        up = lyu[...] * (yu[f, 0] - ylo[f, 0])
        down = lyd[...] * (yd[f, 0] - yhi[f, 0])
        left = lzl[...] * (zl[f] - zlo[f])
        right = lzr[...] * (zr[f] - zhi[f])

        def both(a, first, last):
            return add_last_row(add_first_row(a, first), last)

        oylo[f, 0] = both(pylo[f, 0] + up, left[0:1], right[0:1])
        oyhi[f, 0] = both(pyhi[f, 0] + down, left[ny - 1 : ny], right[ny - 1 : ny])
        ozlo[f] = both(pzlo[f] + left, up[0:1], down[0:1])
        ozhi[f] = both(pzhi[f] + right, up[nz - 1 : nz], down[nz - 1 : nz])


def face_relax(*args):
    nf, _, nz, nx = args[0].shape
    ny = args[2].shape[1]
    full = lambda a: pl.BlockSpec(a.shape, lambda i: (0,) * len(a.shape))
    ys = jax.ShapeDtypeStruct((nf, 1, nz, nx), jnp.float32)
    zs = jax.ShapeDtypeStruct((nf, ny, nx), jnp.float32)
    ly = jax.ShapeDtypeStruct((nz, nx), jnp.float32)
    lz = jax.ShapeDtypeStruct((ny, nx), jnp.float32)
    outs = (ys, ys, zs, zs, ly, ly, lz, lz)
    return pl.pallas_call(
        face_kernel,
        grid=(1,),
        in_specs=[full(a) for a in args],
        out_specs=tuple(full(a) for a in outs),
        out_shape=outs,
        compiler_params=limit(24),
    )(*args)


def again_kernel(p_ref, wx, wy, wz, oylo, oyhi, ozlo, ozhi, t_ref, once):
    ny, nz, _ = wx.shape
    for y in range(ny):
        if y == 0:
            once[y] = oylo[0, 0]
        elif y == ny - 1:
            once[y] = oyhi[0, 0]
        else:
            once[y] = p_ref[0, y]
            once[y, 0:1] = ozlo[0, y : y + 1]
            once[y, nz - 1 : nz] = ozhi[0, y : y + 1]

    def emit(y, c, t):
        t_ref[0, y] = c + t

    relax_slabs(lambda y: once[y], wx, wy, wz, emit)


def specs(nf, ny, nz, nx):
    block = pl.BlockSpec((1, ny, nz, nx), lambda f: (f, 0, 0, 0))
    yface = pl.BlockSpec((1, 1, nz, nx), lambda f: (f, 0, 0, 0))
    zface = pl.BlockSpec((1, ny, nx), lambda f: (f, 0, 0))
    return block, yface, zface


def again_relax(p, wx, wy, wz, *faces):
    nf, ny, nz, nx = p.shape
    block, yface, zface = specs(*p.shape)
    whole = pl.BlockSpec((ny, nz, nx), lambda f: (0, 0, 0))
    return pl.pallas_call(
        again_kernel,
        grid=(nf,),
        in_specs=[block, whole, whole, whole, yface, yface, zface, zface],
        out_specs=block,
        out_shape=jax.ShapeDtypeStruct(p.shape, jnp.float32),
        scratch_shapes=[pltpu.VMEM((ny, nz, nx), jnp.float32)],
        compiler_params=limit(24),
    )(far(p), far(wx), far(wy), far(wz), *faces)


def edge_kernel(
    t_ref, oylo, oyhi, ozlo, ozhi, yu, yd, zl, zr, lyu, lyd, lzl, lzr,
    r_ref, g_ref, high, low,
):
    f = pl.program_id(0)
    _, ny, nz, nx = t_ref.shape
    left = lzl[...] * (zl[0] - ozlo[0])
    right = lzr[...] * (zr[0] - ozhi[0])
    for y in range(ny):
        r = t_ref[0, y]
        if y == 0:
            r = r + lyu[...] * (yu[0, 0] - oylo[0, 0])
        if y == ny - 1:
            r = r + lyd[...] * (yd[0, 0] - oyhi[0, 0])
        r = add_first_row(r, left[y : y + 1])
        r = add_last_row(r, right[y : y + 1])
        r_ref[0, y] = r
        h = r.astype(jnp.bfloat16)
        at = pl.ds(pl.multiple_of(f * (ny * nz) + y * nz, nz), nz)
        high[at] = h
        low[at] = (r - h.astype(jnp.float32)).astype(jnp.bfloat16)

    def cross(a, b):
        return lax.dot_general(a, b, (((0,), (0,)), ((), ())), preferred_element_type=jnp.float32)

    @pl.when(f == pl.num_programs(0) - 1)
    def _():
        half = nx // 2
        part = (slice(0, half), slice(half, nx))
        acc_hh, acc_hl = [], []
        for i in range(3):
            a, b = part[i // 2], part[(i + 1) // 2]
            acc_hh.append(cross(high[:, a], high[:, b]) + cross(low[:, a], low[:, b]))
        for i in range(4):
            acc_hl.append(cross(high[:, part[i // 2]], low[:, part[i % 2]]))
        per = half // BLK

        def inner_block(i, j):
            return slice(i % per * BLK, (i % per + 1) * BLK), slice(j % per * BLK, (j % per + 1) * BLK)

        t = 0
        for i in range(2 * per):
            for j in range(i, 2 * per):
                p, q = i // per, j // per
                a, b = inner_block(i, j)
                g_ref[t] = acc_hh[p + q][a, b] + acc_hl[2 * p + q][a, b] + acc_hl[2 * q + p][b, a].T
                t += 1


def edge_relax(t, faces, halos, links):
    nf, ny, nz, nx = t.shape
    block, yface, zface = specs(*t.shape)
    ly = pl.BlockSpec((nz, nx), lambda f: (0, 0))
    lz = pl.BlockSpec((ny, nx), lambda f: (0, 0))
    cnt = nx // BLK
    nb = cnt * (cnt + 1) // 2
    return pl.pallas_call(
        edge_kernel,
        grid=(nf,),
        in_specs=[block] + [yface, yface, zface, zface] * 2 + [ly, ly, lz, lz],
        out_specs=(block, pl.BlockSpec((nb, BLK, BLK), lambda f: (0, 0, 0))),
        out_shape=(
            pltpu.HBM(t.shape, jnp.float32),
            jax.ShapeDtypeStruct((nb, BLK, BLK), jnp.float32),
        ),
        scratch_shapes=[pltpu.VMEM((nf * ny * nz, nx), jnp.bfloat16)] * 2,
        compiler_params=limit(24),
    )(t, *faces, *halos, *links)


def basis_kernel(r_ref, n_ref, o_ref, high, low):
    @pl.when(pl.program_id(0) == 0)
    def _():
        n = n_ref[...]
        h = n.astype(jnp.bfloat16)
        high[...] = h
        low[...] = (n - h.astype(jnp.float32)).astype(jnp.bfloat16)

    r = r_ref[...]
    a = r.astype(jnp.bfloat16)
    b = (r - a.astype(jnp.float32)).astype(jnp.bfloat16)
    width = r.shape[1]
    step = 256
    for lo in range(0, width, step):
        hi = lo + step

        def times(x, m):
            return lax.dot_general(
                x[:, 0:hi], m[lo:hi, 0:hi], (((1,), (1,)), ((), ())), preferred_element_type=jnp.float32
            )

        o_ref[:, lo:hi] = times(a, high) + (times(a, low) + times(b, high))


def basis_of(rows, inverse_t, chunk=512):
    m, nx = rows.shape
    block = pl.BlockSpec((chunk, nx), lambda i: (i, 0))
    return pl.pallas_call(
        basis_kernel,
        grid=(m // chunk,),
        in_specs=[block, pl.BlockSpec((nx, nx), lambda i: (0, 0))],
        out_specs=block,
        out_shape=jax.ShapeDtypeStruct((m, nx), jnp.float32),
        scratch_shapes=[pltpu.VMEM((nx, nx), jnp.bfloat16)] * 2,
        compiler_params=pltpu.CompilerParams(vmem_limit_bytes=24 * 2**20),
    )(far(rows), inverse_t)

BY = ("yh", "c")
BZ = ("x", "z", "yl")


def axis_count(axes):
    count = 1
    for axis in axes:
        count *= lax.axis_size(axis)
    return count


def from_next(piece, axes, step):
    n = axis_count(axes)
    return lax.ppermute(piece, axes, [(i + step, i) for i in range(n) if 0 <= i + step < n])


def on_device(fields, conductance):
    nfield, ny, nz, width = fields.shape

    def cells(ys, zs):
        return jnp.concatenate([fields[:, ys, zs], conductance[None, ys, zs]], axis=0)

    every = slice(None)
    ylo, yhi = cells(slice(0, 1), every), cells(slice(-1, None), every)
    zlo, zhi = cells(every, 0), cells(every, -1)

    def neighbours(ylo, yhi, zlo, zhi):
        return from_next(yhi, BY, -1), from_next(ylo, BY, 1), from_next(zhi, BZ, -1), from_next(zlo, BZ, 1)

    halo = neighbours(ylo, yhi, zlo, zhi)
    part, wx, wy, wz, *own = own_relax(fields, conductance)
    out = face_relax(*own, ylo, yhi, zlo, zhi, *halo)
    faces, links = out[:4], out[4:]
    halo = neighbours(*faces)
    twice = again_relax(part, wx, wy, wz, *faces)
    relaxed, blocks = edge_relax(twice, faces, halo, links)
    total_rows = nfield * ny * axis_count(BY) * nz * axis_count(BZ)
    blocks = sum_over_devices(blocks) / jnp.float32(total_rows)
    factor, inverse_t = factor_and_inverse(blocks, width)
    basis = basis_of(relaxed.reshape(-1, width), inverse_t)
    return (basis.reshape(relaxed.shape), factor)


def solution(mesh):
    fine = Mesh(mesh.devices.reshape(2, 2, 4, 4, 2), ("yh", "c", "x", "z", "yl"))
    return jax.shard_map(
        on_device,
        mesh=fine,
        in_specs=(P(None, BY, BZ, None), P(BY, BZ, None)),
        out_specs=(P(None, BY, BZ, None), P()),
        check_vma=False,
    )
```

```python
import jax
import jax.numpy as jnp
from jax import lax
from jax.experimental import pallas as pl
from jax.experimental.pallas import tpu as pltpu
from jax.sharding import Mesh, PartitionSpec as P

HI = lax.Precision.HIGHEST
BLK = 128
PAN = 32
Y_AXES = ("yh", "yl")

def shifted(piece, axes, count, distance):
    return lax.ppermute(piece, axes, [(i, (i + distance) % count) for i in range(count)])


def scatter_sum(pieces, axes, count):
    me = lax.axis_index(axes)
    own = lax.dynamic_index_in_dim(pieces, me, 0, keepdims=False)
    for d in range(1, count):
        send = lax.dynamic_index_in_dim(pieces, (me + d) % count, 0, keepdims=False)
        own = own + shifted(send, axes, count, d)
    return own


def gather(piece, axes, count):
    me = lax.axis_index(axes)
    out = jnp.zeros((count,) + piece.shape, piece.dtype)
    for d in range(count):
        part = piece if d == 0 else shifted(piece, axes, count, d)
        out = lax.dynamic_update_index_in_dim(out, part, (me - d) % count, 0)
    return out


def exchange_sum(piece, axes, count):
    total = piece
    for d in range(1, count):
        total = total + shifted(piece, axes, count, d)
    return total


def sum_over_devices(blocks):
    shape = blocks.shape
    x = blocks.reshape(2, 4, -1, shape[-1])
    x = scatter_sum(x, ("c",), 2)
    x = scatter_sum(x, Y_AXES, 4)
    x = exchange_sum(x, ("z",), 4)
    x = exchange_sum(x, ("x",), 4)
    x = gather(x, Y_AXES, 4)
    x = gather(x, ("c",), 2)
    return x.reshape(shape)


def rows_of(x,k):
    return jnp.broadcast_to(x[k:k+1,:],(8,x.shape[1]))

def diag_factor(work, PAN=PAN):
    nt=PAN//8
    iota=lax.broadcasted_iota(jnp.int32,(8,128),0)
    for p in range(BLK//PAN):
        j=p*PAN
        left=[work[j+8*t:j+8*t+8,0:128] for t in range(nt)]
        right=[work[j+8*t:j+8*t+8,128:256] for t in range(nt)]
        cols=[[jnp.broadcast_to(left[t][:,j+k:j+k+1],(8,128)) for t in range(nt)] for k in range(PAN)]
        scale=[jnp.zeros((8,128),jnp.float32) for _ in range(nt)]
        for k in range(PAN):
            t0,s0=k//8,k%8
            d=rows_of(cols[k][t0],s0)
            inv=1.0/d
            scale[t0]=jnp.where(iota==s0,lax.rsqrt(d),scale[t0])
            coef=[None]*nt
            for t in range(t0,nt):
                c=cols[k][t]*inv
                if t==t0: c=jnp.where(iota>s0,c,0.0)
                coef[t]=c
            for m in range(k+1,PAN):
                b=rows_of(cols[m][t0],s0)
                for t in range(t0,nt):
                    cols[m][t]=cols[m][t]-coef[t]*b
            for arr in (left,right):
                b=rows_of(arr[t0],s0)
                for t in range(t0,nt):
                    arr[t]=arr[t]-coef[t]*b
        left=[l*s for l,s in zip(left,scale)]
        right=[l*s for l,s in zip(right,scale)]
        for t in range(nt):
            work[j+8*t:j+8*t+8,0:128]=left[t]
            work[j+8*t:j+8*t+8,128:256]=right[t]
        if j+PAN<BLK:
            L=jnp.concatenate(left,0)
            R=jnp.concatenate([L,jnp.concatenate(right,0)],1)
            up=lax.dot_general(L,R,(((0,),(0,)),((),())),precision=HI,preferred_element_type=jnp.float32)
            work[j+PAN:BLK,:]=work[j+PAN:BLK,:]-up[j+PAN:BLK,:]

def factor_kernel(g_ref,fac_ref,n_ref,work):
    n=n_ref.shape[0]
    cnt=n//BLK
    t=0
    for i in range(cnt):
        for j in range(i,cnt):
            n_ref[i*BLK:(i+1)*BLK,j*BLK:(j+1)*BLK]=g_ref[t]
            t+=1
    r=lax.broadcasted_iota(jnp.int32,(BLK,BLK),0)
    c=lax.broadcasted_iota(jnp.int32,(BLK,BLK),1)
    for k in range(cnt):
        lo,hi=k*BLK,(k+1)*BLK
        work[:,0:128]=n_ref[lo:hi,lo:hi]
        work[:,128:256]=jnp.where(r==c,1.0,0.0)
        diag_factor(work)
        rkk=jnp.where(r<=c,work[:,0:128],0.0)
        m=jnp.where(r>=c,work[:,128:256],0.0)
        fac_ref[lo:hi,lo:hi]=rkk
        if lo>0:
            fac_ref[lo:hi,0:lo]=jnp.zeros((BLK,lo),jnp.float32)
            n_ref[lo:hi,0:lo]=jnp.dot(m,n_ref[lo:hi,0:lo],precision=HI,preferred_element_type=jnp.float32)
        n_ref[lo:hi,lo:hi]=m
        if hi<n:
            rk=jnp.dot(m,n_ref[lo:hi,hi:n],precision=HI,preferred_element_type=jnp.float32)
            fac_ref[lo:hi,hi:n]=rk
            n_ref[lo:hi,hi:n]=jnp.zeros((BLK,n-hi),jnp.float32)
            upn=lax.dot_general(rk,n_ref[lo:hi,0:hi],(((0,),(0,)),((),())),precision=HI,preferred_element_type=jnp.float32)
            if lo>0: n_ref[hi:n,0:lo]=n_ref[hi:n,0:lo]-upn[:,0:lo]
            n_ref[hi:n,lo:hi]=-upn[:,lo:hi]
            upw=lax.dot_general(rk,rk,(((0,),(0,)),((),())),precision=HI,preferred_element_type=jnp.float32)
            for i in range(k+1,cnt):
                a=i*BLK
                n_ref[a:a+BLK,a:n]=n_ref[a:a+BLK,a:n]-upw[a-hi:a-hi+BLK,a-hi:]


def factor_and_inverse(blocks, n):
    square = jax.ShapeDtypeStruct((n, n), jnp.float32)
    whole = pl.BlockSpec(memory_space=pltpu.VMEM)
    return pl.pallas_call(
        factor_kernel,
        out_shape=(square, square),
        in_specs=[whole],
        out_specs=(whole, whole),
        scratch_shapes=[pltpu.VMEM((BLK, 2 * BLK), jnp.float32)],
        compiler_params=pltpu.CompilerParams(vmem_limit_bytes=24 * 2**20),
    )(blocks)


def ahead(a, axis):
    return pltpu.roll(a, a.shape[axis] - 1, axis)


def behind(a, axis):
    return pltpu.roll(a, 1, axis)


def link(a, b):
    return 0.125 * jnp.sqrt(a * b)


def link_along(k, axis):
    n = k.shape[axis]
    at = lax.broadcasted_iota(jnp.int32, k.shape, axis)
    return jnp.where(at < n - 1, link(k, ahead(k, axis)), 0.0)


def flow_along(u, w, axis):
    flux = w * (ahead(u, axis) - u)
    return flux - behind(flux, axis)


def add_first_row(a, row):
    top = a[0:8]
    at = lax.broadcasted_iota(jnp.int32, top.shape, 0)
    top = top + jnp.where(at == 0, jnp.broadcast_to(row, top.shape), 0.0)
    return jnp.concatenate([top, a[8:]], 0)


def add_last_row(a, row):
    n = a.shape[0]
    end = a[n - 8 :]
    at = lax.broadcasted_iota(jnp.int32, end.shape, 0)
    end = end + jnp.where(at == 7, jnp.broadcast_to(row, end.shape), 0.0)
    return jnp.concatenate([a[: n - 8], end], 0)


def flow_both(u, w, wb):
    return w * (ahead(u, 1) - u) + wb * (behind(u, 1) - u)


def relax_slabs(u, wx, wxb, wy, wz, emit):
    count = wx.shape[0]
    below = None
    for y in range(count):
        c = u(y)
        t = flow_both(c, wx[y], wxb[y]) + flow_along(c, wz[y], 0)
        if below is not None:
            t = t - below
        if y + 1 < count:
            below = wy[y] * (u(y + 1) - c)
            t = t + below
        emit(y, c, t)


DEPTH = 4
FAR = pl.BlockSpec(memory_space=pltpu.HBM)
NEAR = pl.BlockSpec(memory_space=pltpu.VMEM)


def far(x):
    return pltpu.with_memory_space_constraint(x, pltpu.HBM)


def limit(mib):
    return pltpu.CompilerParams(vmem_limit_bytes=mib * 2**20)


def stream(count, fetch, work, store):
    if fetch is not None:
        for i in range(min(DEPTH, count)):
            fetch(i).start()

    def step(i, carry):
        if fetch is not None:
            fetch(i).wait()

            @pl.when(i + DEPTH < count)
            def _():
                fetch(i + DEPTH).start()

        work(i)
        if store is not None:
            store(i).start()
        return carry

    lax.fori_loop(0, count, step, 0)


def drain(count, store):
    for i in range(count):
        store(i).wait()


def own_kernel(
    f_far, k_far, p_far, wx_far, wy_far, wz_far, pylo, pyhi, pzlo, pzhi,
    fbuf, k_ref, pbuf, wx, wxb, wy, wz, f_sem, p_sem, k_sem, w_sem,
):
    nf, count, nz, _ = fbuf.shape
    k_copy = pltpu.make_async_copy(k_far, k_ref, k_sem)
    k_copy.start()
    w_copies = [
        pltpu.make_async_copy(a, b, w_sem.at[i])
        for i, (a, b) in enumerate(((wx, wx_far), (wy, wy_far), (wz, wz_far)))
    ]

    def fetch(f):
        return pltpu.make_async_copy(f_far.at[f], fbuf.at[f], f_sem.at[f])

    def store(f):
        return pltpu.make_async_copy(pbuf.at[f], p_far.at[f], p_sem.at[f])

    def work(f):
        @pl.when(f == 0)
        def _():
            k_copy.wait()
            for y in range(count):
                k = k_ref[y]
                w = link_along(k, 1)
                wx[y] = w
                wxb[y] = behind(w, 1)
                wz[y] = link_along(k, 0)
                wy[y] = link(k, k_ref[y + 1]) if y + 1 < count else jnp.zeros_like(k)
            for c in w_copies:
                c.start()

        def emit(y, c, t):
            r = c + t
            pbuf[f, y] = r
            if y == 0:
                pylo[f, 0] = r
            if y == count - 1:
                pyhi[f, 0] = r
            pzlo[f, y : y + 1] = r[0:1]
            pzhi[f, y : y + 1] = r[nz - 1 : nz]

        relax_slabs(lambda y: fbuf[f, y], wx, wxb, wy, wz, emit)

    stream(nf, fetch, work, store)
    drain(nf, store)
    for c in w_copies:
        c.wait()


def own_relax(fields, conductance):
    nf, ny, nz, nx = fields.shape
    w = pltpu.HBM((ny, nz, nx), jnp.float32)
    yf = jax.ShapeDtypeStruct((nf, 1, nz, nx), jnp.float32)
    zf = jax.ShapeDtypeStruct((nf, ny, nx), jnp.float32)
    big = pltpu.VMEM(fields.shape, jnp.float32)
    one = pltpu.VMEM((ny, nz, nx), jnp.float32)
    sem = pltpu.SemaphoreType.DMA
    return pl.pallas_call(
        own_kernel,
        in_specs=[FAR, FAR],
        out_specs=(FAR,) * 4 + (NEAR,) * 4,
        out_shape=(pltpu.HBM(fields.shape, jnp.float32), w, w, w, yf, yf, zf, zf),
        scratch_shapes=[big, one, big, one, one, one, one, sem((nf,)), sem((nf,)), sem, sem((3,))],
        compiler_params=limit(32),
    )(far(fields), far(conductance))


def face_kernel(
    pylo, pyhi, pzlo, pzhi, ylo, yhi, zlo, zhi, yu, yd, zl, zr,
    oylo, oyhi, ozlo, ozhi, lyu, lyd, lzl, lzr,
):
    nf, _, nz, _ = pylo.shape
    ny = pzlo.shape[1]
    lyu[...] = link(ylo[nf, 0], yu[nf, 0])
    lyd[...] = link(yhi[nf, 0], yd[nf, 0])
    lzl[...] = link(zlo[nf], zl[nf])
    lzr[...] = link(zhi[nf], zr[nf])
    for f in range(nf):
        up = lyu[...] * (yu[f, 0] - ylo[f, 0])
        down = lyd[...] * (yd[f, 0] - yhi[f, 0])
        left = lzl[...] * (zl[f] - zlo[f])
        right = lzr[...] * (zr[f] - zhi[f])

        def both(a, first, last):
            return add_last_row(add_first_row(a, first), last)

        oylo[f, 0] = both(pylo[f, 0] + up, left[0:1], right[0:1])
        oyhi[f, 0] = both(pyhi[f, 0] + down, left[ny - 1 : ny], right[ny - 1 : ny])
        ozlo[f] = both(pzlo[f] + left, up[0:1], down[0:1])
        ozhi[f] = both(pzhi[f] + right, up[nz - 1 : nz], down[nz - 1 : nz])


def face_relax(*args):
    nf, _, nz, nx = args[0].shape
    ny = args[2].shape[1]
    full = lambda a: pl.BlockSpec(a.shape, lambda i: (0,) * len(a.shape))
    ys = jax.ShapeDtypeStruct((nf, 1, nz, nx), jnp.float32)
    zs = jax.ShapeDtypeStruct((nf, ny, nx), jnp.float32)
    ly = jax.ShapeDtypeStruct((nz, nx), jnp.float32)
    lz = jax.ShapeDtypeStruct((ny, nx), jnp.float32)
    outs = (ys, ys, zs, zs, ly, ly, lz, lz)
    return pl.pallas_call(
        face_kernel,
        grid=(1,),
        in_specs=[full(a) for a in args],
        out_specs=tuple(full(a) for a in outs),
        out_shape=outs,
        compiler_params=limit(24),
    )(*args)


def again_kernel(
    p_far, wx_far, wy_far, wz_far, oylo, oyhi, ozlo, ozhi, t_ref, once, wx, wxb, wy, wz, p_sem, w_sem
):
    nf, ny, nz, _ = once.shape
    w_copies = [
        pltpu.make_async_copy(a, b, w_sem.at[i])
        for i, (a, b) in enumerate(((wx_far, wx), (wy_far, wy), (wz_far, wz)))
    ]
    for c in w_copies:
        c.start()

    def fetch(f):
        return pltpu.make_async_copy(p_far.at[f], once.at[f], p_sem.at[f])

    def work(f):
        @pl.when(f == 0)
        def _():
            for c in w_copies:
                c.wait()
            for y in range(ny):
                wxb[y] = behind(wx[y], 1)

        once[f, 0] = oylo[f, 0]
        once[f, ny - 1] = oyhi[f, 0]
        for y in range(1, ny - 1):
            once[f, y, 0:1] = ozlo[f, y : y + 1]
            once[f, y, nz - 1 : nz] = ozhi[f, y : y + 1]

        def emit(y, c, t):
            t_ref[f, y] = c + t

        relax_slabs(lambda y: once[f, y], wx, wxb, wy, wz, emit)

    stream(nf, fetch, work, None)


def again_relax(p, wx, wy, wz, *faces):
    nf, ny, nz, nx = p.shape
    one = pltpu.VMEM((ny, nz, nx), jnp.float32)
    sem = pltpu.SemaphoreType.DMA
    return pl.pallas_call(
        again_kernel,
        in_specs=[FAR] * 4 + [NEAR] * 4,
        out_specs=NEAR,
        out_shape=jax.ShapeDtypeStruct(p.shape, jnp.float32),
        scratch_shapes=[pltpu.VMEM(p.shape, jnp.float32), one, one, one, one, sem((nf,)), sem((3,))],
        compiler_params=limit(32),
    )(far(p), far(wx), far(wy), far(wz), *faces)


def edge_kernel(
    t_ref, oylo, oyhi, ozlo, ozhi, yu, yd, zl, zr, lyu, lyd, lzl, lzr,
    r_far, g_ref, rbuf, high, low, r_sem,
):
    nf, ny, nz, nx = t_ref.shape

    def store(f):
        return pltpu.make_async_copy(rbuf.at[f], r_far.at[f], r_sem.at[f])

    def work(f):
        left = lzl[...] * (zl[f] - ozlo[f])
        right = lzr[...] * (zr[f] - ozhi[f])
        for y in range(ny):
            r = t_ref[f, y]
            if y == 0:
                r = r + lyu[...] * (yu[f, 0] - oylo[f, 0])
            if y == ny - 1:
                r = r + lyd[...] * (yd[f, 0] - oyhi[f, 0])
            r = add_first_row(r, left[y : y + 1])
            r = add_last_row(r, right[y : y + 1])
            rbuf[f, y] = r
            h = r.astype(jnp.bfloat16)
            at = pl.ds(pl.multiple_of(f * (ny * nz) + y * nz, nz), nz)
            high[at] = h
            low[at] = (r - h.astype(jnp.float32)).astype(jnp.bfloat16)

    stream(nf, None, work, store)

    def cross(a, b):
        return lax.dot_general(a, b, (((0,), (0,)), ((), ())), preferred_element_type=jnp.float32)

    half = nx // 2
    part = (slice(0, half), slice(half, nx))
    acc_hh, acc_hl = [], []
    for i in range(3):
        a, b = part[i // 2], part[(i + 1) // 2]
        acc_hh.append(cross(high[:, a], high[:, b]) + cross(low[:, a], low[:, b]))
    for i in range(4):
        acc_hl.append(cross(high[:, part[i // 2]], low[:, part[i % 2]]))
    per = half // BLK

    def inner_block(i, j):
        return slice(i % per * BLK, (i % per + 1) * BLK), slice(j % per * BLK, (j % per + 1) * BLK)

    t = 0
    for i in range(2 * per):
        for j in range(i, 2 * per):
            p, q = i // per, j // per
            a, b = inner_block(i, j)
            g_ref[t] = acc_hh[p + q][a, b] + acc_hl[2 * p + q][a, b] + acc_hl[2 * q + p][b, a].T
            t += 1

    drain(nf, store)


def edge_relax(t, faces, halos, links):
    nf, ny, nz, nx = t.shape
    cnt = nx // BLK
    nb = cnt * (cnt + 1) // 2
    return pl.pallas_call(
        edge_kernel,
        in_specs=[NEAR] * 13,
        out_specs=(FAR, NEAR),
        out_shape=(
            pltpu.HBM(t.shape, jnp.float32),
            jax.ShapeDtypeStruct((nb, BLK, BLK), jnp.float32),
        ),
        scratch_shapes=[pltpu.VMEM(t.shape, jnp.float32)]
        + [pltpu.VMEM((nf * ny * nz, nx), jnp.bfloat16)] * 2
        + [pltpu.SemaphoreType.DMA((nf,))],
        compiler_params=limit(32),
    )(t, *faces, *halos, *links)


def basis_kernel(r_far, n_ref, o_far, rbuf, obuf, high, low, r_sem, o_sem):
    count, chunk, width = rbuf.shape
    step = 256

    def fetch(i):
        return pltpu.make_async_copy(r_far.at[i], rbuf.at[i], r_sem.at[i])

    def store(i):
        return pltpu.make_async_copy(obuf.at[i], o_far.at[i], o_sem.at[i])

    def work(i):
        @pl.when(i == 0)
        def _():
            n = n_ref[...]
            h = n.astype(jnp.bfloat16)
            high[...] = h
            low[...] = (n - h.astype(jnp.float32)).astype(jnp.bfloat16)

        r = rbuf[i]
        a = r.astype(jnp.bfloat16)
        b = (r - a.astype(jnp.float32)).astype(jnp.bfloat16)
        for lo in range(0, width, step):
            hi = lo + step

            def times(x, m):
                return lax.dot_general(
                    x[:, 0:hi], m[lo:hi, 0:hi], (((1,), (1,)), ((), ())), preferred_element_type=jnp.float32
                )

            obuf[i, :, lo:hi] = times(a, high) + (times(a, low) + times(b, high))

    stream(count, fetch, work, store)
    drain(count, store)


def basis_of(rows, inverse_t, chunk=512):
    m, nx = rows.shape
    cut = (m // chunk, chunk, nx)
    big = pltpu.VMEM(cut, jnp.float32)
    sem = pltpu.SemaphoreType.DMA((m // chunk,))
    return pl.pallas_call(
        basis_kernel,
        in_specs=[FAR, NEAR],
        out_specs=FAR,
        out_shape=pltpu.HBM(cut, jnp.float32),
        scratch_shapes=[big, big] + [pltpu.VMEM((nx, nx), jnp.bfloat16)] * 2 + [sem, sem],
        compiler_params=limit(32),
    )(far(rows.reshape(cut)), inverse_t)


BY = ("yh", "c")
BZ = ("x", "z", "yl")


def axis_count(axes):
    count = 1
    for axis in axes:
        count *= lax.axis_size(axis)
    return count


def from_next(piece, axes, step):
    n = axis_count(axes)
    return lax.ppermute(piece, axes, [(i + step, i) for i in range(n) if 0 <= i + step < n])


def on_device(fields, conductance):
    nfield, ny, nz, width = fields.shape

    def cells(ys, zs):
        return jnp.concatenate([fields[:, ys, zs], conductance[None, ys, zs]], axis=0)

    every = slice(None)
    ylo, yhi = cells(slice(0, 1), every), cells(slice(-1, None), every)
    zlo, zhi = cells(every, 0), cells(every, -1)

    def neighbours(ylo, yhi, zlo, zhi):
        return from_next(yhi, BY, -1), from_next(ylo, BY, 1), from_next(zhi, BZ, -1), from_next(zlo, BZ, 1)

    halo = neighbours(ylo, yhi, zlo, zhi)
    part, wx, wy, wz, *own = own_relax(fields, conductance)
    out = face_relax(*own, ylo, yhi, zlo, zhi, *halo)
    faces, links = out[:4], out[4:]
    halo = neighbours(*faces)
    twice = again_relax(part, wx, wy, wz, *faces)
    relaxed, blocks = edge_relax(twice, faces, halo, links)
    total_rows = nfield * ny * axis_count(BY) * nz * axis_count(BZ)
    blocks = sum_over_devices(blocks) / jnp.float32(total_rows)
    factor, inverse_t = factor_and_inverse(blocks, width)
    basis = basis_of(relaxed.reshape(-1, width), inverse_t)
    return (basis.reshape(relaxed.shape), factor)


def solution(mesh):
    fine = Mesh(mesh.devices.reshape(2, 2, 4, 4, 2), ("yh", "c", "x", "z", "yl"))
    return jax.shard_map(
        on_device,
        mesh=fine,
        in_specs=(P(None, BY, BZ, None), P(BY, BZ, None)),
        out_specs=(P(None, BY, BZ, None), P()),
        check_vma=False,
    )
```

```python
import jax
import jax.numpy as jnp
from jax import lax
from jax.experimental import pallas as pl
from jax.experimental.pallas import tpu as pltpu
from jax.sharding import Mesh, PartitionSpec as P

HI = lax.Precision.HIGHEST
BLK = 128
PAN = 32
Y_AXES = ("yh", "yl")

def shifted(piece, axes, count, distance):
    return lax.ppermute(piece, axes, [(i, (i + distance) % count) for i in range(count)])


def scatter_sum(pieces, axes, count):
    me = lax.axis_index(axes)
    own = lax.dynamic_index_in_dim(pieces, me, 0, keepdims=False)
    for d in range(1, count):
        send = lax.dynamic_index_in_dim(pieces, (me + d) % count, 0, keepdims=False)
        own = own + shifted(send, axes, count, d)
    return own


def gather(piece, axes, count):
    me = lax.axis_index(axes)
    out = jnp.zeros((count,) + piece.shape, piece.dtype)
    for d in range(count):
        part = piece if d == 0 else shifted(piece, axes, count, d)
        out = lax.dynamic_update_index_in_dim(out, part, (me - d) % count, 0)
    return out


def exchange_sum(piece, axes, count):
    total = piece
    for d in range(1, count):
        total = total + shifted(piece, axes, count, d)
    return total


def sum_over_devices(blocks):
    shape = blocks.shape
    x = blocks.reshape(2, 4, -1, shape[-1])
    x = scatter_sum(x, ("c",), 2)
    x = scatter_sum(x, Y_AXES, 4)
    x = exchange_sum(x, ("z",), 4)
    x = exchange_sum(x, ("x",), 4)
    x = gather(x, Y_AXES, 4)
    x = gather(x, ("c",), 2)
    return x.reshape(shape)


def rows_of(x,k):
    return jnp.broadcast_to(x[k:k+1,:],(8,x.shape[1]))

def diag_factor(work, PAN=PAN):
    nt=PAN//8
    iota=lax.broadcasted_iota(jnp.int32,(8,128),0)
    for p in range(BLK//PAN):
        j=p*PAN
        left=[work[j+8*t:j+8*t+8,0:128] for t in range(nt)]
        right=[work[j+8*t:j+8*t+8,128:256] for t in range(nt)]
        cols=[[jnp.broadcast_to(left[t][:,j+k:j+k+1],(8,128)) for t in range(nt)] for k in range(PAN)]
        scale=[jnp.zeros((8,128),jnp.float32) for _ in range(nt)]
        for k in range(PAN):
            t0,s0=k//8,k%8
            d=rows_of(cols[k][t0],s0)
            inv=1.0/d
            scale[t0]=jnp.where(iota==s0,lax.rsqrt(d),scale[t0])
            coef=[None]*nt
            for t in range(t0,nt):
                c=cols[k][t]*inv
                if t==t0: c=jnp.where(iota>s0,c,0.0)
                coef[t]=c
            for m in range(k+1,PAN):
                b=rows_of(cols[m][t0],s0)
                for t in range(t0,nt):
                    cols[m][t]=cols[m][t]-coef[t]*b
            for arr in (left,right):
                b=rows_of(arr[t0],s0)
                for t in range(t0,nt):
                    arr[t]=arr[t]-coef[t]*b
        left=[l*s for l,s in zip(left,scale)]
        right=[l*s for l,s in zip(right,scale)]
        for t in range(nt):
            work[j+8*t:j+8*t+8,0:128]=left[t]
            work[j+8*t:j+8*t+8,128:256]=right[t]
        if j+PAN<BLK:
            L=jnp.concatenate(left,0)
            R=jnp.concatenate([L,jnp.concatenate(right,0)],1)
            up=lax.dot_general(L,R,(((0,),(0,)),((),())),precision=HI,preferred_element_type=jnp.float32)
            work[j+PAN:BLK,:]=work[j+PAN:BLK,:]-up[j+PAN:BLK,:]

def factor_kernel(g_ref,fac_ref,n_ref,work):
    n=n_ref.shape[0]
    cnt=n//BLK
    t=0
    for i in range(cnt):
        for j in range(i,cnt):
            n_ref[i*BLK:(i+1)*BLK,j*BLK:(j+1)*BLK]=g_ref[t]
            t+=1
    r=lax.broadcasted_iota(jnp.int32,(BLK,BLK),0)
    c=lax.broadcasted_iota(jnp.int32,(BLK,BLK),1)
    for k in range(cnt):
        lo,hi=k*BLK,(k+1)*BLK
        work[:,0:128]=n_ref[lo:hi,lo:hi]
        work[:,128:256]=jnp.where(r==c,1.0,0.0)
        diag_factor(work)
        rkk=jnp.where(r<=c,work[:,0:128],0.0)
        m=jnp.where(r>=c,work[:,128:256],0.0)
        fac_ref[lo:hi,lo:hi]=rkk
        if lo>0:
            fac_ref[lo:hi,0:lo]=jnp.zeros((BLK,lo),jnp.float32)
            n_ref[lo:hi,0:lo]=jnp.dot(m,n_ref[lo:hi,0:lo],precision=HI,preferred_element_type=jnp.float32)
        n_ref[lo:hi,lo:hi]=m
        if hi<n:
            rk=jnp.dot(m,n_ref[lo:hi,hi:n],precision=HI,preferred_element_type=jnp.float32)
            fac_ref[lo:hi,hi:n]=rk
            n_ref[lo:hi,hi:n]=jnp.zeros((BLK,n-hi),jnp.float32)
            upn=lax.dot_general(rk,n_ref[lo:hi,0:hi],(((0,),(0,)),((),())),precision=HI,preferred_element_type=jnp.float32)
            if lo>0: n_ref[hi:n,0:lo]=n_ref[hi:n,0:lo]-upn[:,0:lo]
            n_ref[hi:n,lo:hi]=-upn[:,lo:hi]
            upw=lax.dot_general(rk,rk,(((0,),(0,)),((),())),precision=HI,preferred_element_type=jnp.float32)
            for i in range(k+1,cnt):
                a=i*BLK
                n_ref[a:a+BLK,a:n]=n_ref[a:a+BLK,a:n]-upw[a-hi:a-hi+BLK,a-hi:]


def ahead(a, axis):
    return pltpu.roll(a, a.shape[axis] - 1, axis)


def behind(a, axis):
    return pltpu.roll(a, 1, axis)


def link(a, b):
    return 0.125 * jnp.sqrt(a * b)


def link_along(k, axis):
    n = k.shape[axis]
    at = lax.broadcasted_iota(jnp.int32, k.shape, axis)
    return jnp.where(at < n - 1, link(k, ahead(k, axis)), 0.0)


def flow_along(u, w, axis):
    flux = w * (ahead(u, axis) - u)
    return flux - behind(flux, axis)


def add_first_row(a, row):
    top = a[0:8]
    at = lax.broadcasted_iota(jnp.int32, top.shape, 0)
    top = top + jnp.where(at == 0, jnp.broadcast_to(row, top.shape), 0.0)
    return jnp.concatenate([top, a[8:]], 0)


def add_last_row(a, row):
    n = a.shape[0]
    end = a[n - 8 :]
    at = lax.broadcasted_iota(jnp.int32, end.shape, 0)
    end = end + jnp.where(at == 7, jnp.broadcast_to(row, end.shape), 0.0)
    return jnp.concatenate([a[: n - 8], end], 0)


def flow_both(u, w, wb):
    return w * (ahead(u, 1) - u) + wb * (behind(u, 1) - u)


def relax_slabs(u, wx, wxb, wy, wz, emit):
    count = wx.shape[0]
    below = None
    for y in range(count):
        c = u(y)
        t = flow_both(c, wx[y], wxb[y]) + flow_along(c, wz[y], 0)
        if below is not None:
            t = t - below
        if y + 1 < count:
            below = wy[y] * (u(y + 1) - c)
            t = t + below
        emit(y, c, t)


DEPTH = 4
FAR = pl.BlockSpec(memory_space=pltpu.HBM)
NEAR = pl.BlockSpec(memory_space=pltpu.VMEM)


def far(x):
    return pltpu.with_memory_space_constraint(x, pltpu.HBM)


def limit(mib):
    return pltpu.CompilerParams(vmem_limit_bytes=mib * 2**20)


def stream(count, fetch, work, store):
    if fetch is not None:
        for i in range(min(DEPTH, count)):
            fetch(i).start()

    def step(i, carry):
        if fetch is not None:
            fetch(i).wait()

            @pl.when(i + DEPTH < count)
            def _():
                fetch(i + DEPTH).start()

        work(i)
        if store is not None:
            store(i).start()
        return carry

    lax.fori_loop(0, count, step, 0)


def drain(count, store):
    for i in range(count):
        store(i).wait()


def own_kernel(
    f_far, k_far, p_far, wx_far, wy_far, wz_far, pylo, pyhi, pzlo, pzhi,
    fbuf, k_ref, pbuf, wx, wxb, wy, wz, f_sem, p_sem, k_sem, w_sem,
):
    nf, count, nz, _ = fbuf.shape
    k_copy = pltpu.make_async_copy(k_far, k_ref, k_sem)
    k_copy.start()
    w_copies = [
        pltpu.make_async_copy(a, b, w_sem.at[i])
        for i, (a, b) in enumerate(((wx, wx_far), (wy, wy_far), (wz, wz_far)))
    ]

    def fetch(f):
        return pltpu.make_async_copy(f_far.at[f], fbuf.at[f], f_sem.at[f])

    def store(f):
        return pltpu.make_async_copy(pbuf.at[f], p_far.at[f], p_sem.at[f])

    def work(f):
        @pl.when(f == 0)
        def _():
            k_copy.wait()
            for y in range(count):
                k = k_ref[y]
                w = link_along(k, 1)
                wx[y] = w
                wxb[y] = behind(w, 1)
                wz[y] = link_along(k, 0)
                wy[y] = link(k, k_ref[y + 1]) if y + 1 < count else jnp.zeros_like(k)
            for c in w_copies:
                c.start()

        def emit(y, c, t):
            r = c + t
            pbuf[f, y] = r
            if y == 0:
                pylo[f, 0] = r
            if y == count - 1:
                pyhi[f, 0] = r
            pzlo[f, y : y + 1] = r[0:1]
            pzhi[f, y : y + 1] = r[nz - 1 : nz]

        relax_slabs(lambda y: fbuf[f, y], wx, wxb, wy, wz, emit)

    stream(nf, fetch, work, store)
    drain(nf, store)
    for c in w_copies:
        c.wait()


def own_relax(fields, conductance):
    nf, ny, nz, nx = fields.shape
    w = pltpu.HBM((ny, nz, nx), jnp.float32)
    yf = jax.ShapeDtypeStruct((nf, 1, nz, nx), jnp.float32)
    zf = jax.ShapeDtypeStruct((nf, ny, nx), jnp.float32)
    big = pltpu.VMEM(fields.shape, jnp.float32)
    one = pltpu.VMEM((ny, nz, nx), jnp.float32)
    sem = pltpu.SemaphoreType.DMA
    return pl.pallas_call(
        own_kernel,
        in_specs=[FAR, FAR],
        out_specs=(FAR,) * 4 + (NEAR,) * 4,
        out_shape=(pltpu.HBM(fields.shape, jnp.float32), w, w, w, yf, yf, zf, zf),
        scratch_shapes=[big, one, big, one, one, one, one, sem((nf,)), sem((nf,)), sem, sem((3,))],
        compiler_params=limit(32),
    )(far(fields), far(conductance))


def face_kernel(
    pylo, pyhi, pzlo, pzhi, ylo, yhi, zlo, zhi, yu, yd, zl, zr,
    oylo, oyhi, ozlo, ozhi, lyu, lyd, lzl, lzr,
):
    nf, _, nz, _ = pylo.shape
    ny = pzlo.shape[1]
    lyu[...] = link(ylo[nf, 0], yu[nf, 0])
    lyd[...] = link(yhi[nf, 0], yd[nf, 0])
    lzl[...] = link(zlo[nf], zl[nf])
    lzr[...] = link(zhi[nf], zr[nf])
    for f in range(nf):
        up = lyu[...] * (yu[f, 0] - ylo[f, 0])
        down = lyd[...] * (yd[f, 0] - yhi[f, 0])
        left = lzl[...] * (zl[f] - zlo[f])
        right = lzr[...] * (zr[f] - zhi[f])

        def both(a, first, last):
            return add_last_row(add_first_row(a, first), last)

        oylo[f, 0] = both(pylo[f, 0] + up, left[0:1], right[0:1])
        oyhi[f, 0] = both(pyhi[f, 0] + down, left[ny - 1 : ny], right[ny - 1 : ny])
        ozlo[f] = both(pzlo[f] + left, up[0:1], down[0:1])
        ozhi[f] = both(pzhi[f] + right, up[nz - 1 : nz], down[nz - 1 : nz])


def face_relax(*args):
    nf, _, nz, nx = args[0].shape
    ny = args[2].shape[1]
    full = lambda a: pl.BlockSpec(a.shape, lambda i: (0,) * len(a.shape))
    ys = jax.ShapeDtypeStruct((nf, 1, nz, nx), jnp.float32)
    zs = jax.ShapeDtypeStruct((nf, ny, nx), jnp.float32)
    ly = jax.ShapeDtypeStruct((nz, nx), jnp.float32)
    lz = jax.ShapeDtypeStruct((ny, nx), jnp.float32)
    outs = (ys, ys, zs, zs, ly, ly, lz, lz)
    return pl.pallas_call(
        face_kernel,
        grid=(1,),
        in_specs=[full(a) for a in args],
        out_specs=tuple(full(a) for a in outs),
        out_shape=outs,
        compiler_params=limit(24),
    )(*args)


def again_kernel(
    p_far, wx_far, wy_far, wz_far, oylo, oyhi, ozlo, ozhi, t_ref, once, wx, wxb, wy, wz, p_sem, w_sem
):
    nf, ny, nz, _ = once.shape
    w_copies = [
        pltpu.make_async_copy(a, b, w_sem.at[i])
        for i, (a, b) in enumerate(((wx_far, wx), (wy_far, wy), (wz_far, wz)))
    ]
    for c in w_copies:
        c.start()

    def fetch(f):
        return pltpu.make_async_copy(p_far.at[f], once.at[f], p_sem.at[f])

    def work(f):
        @pl.when(f == 0)
        def _():
            for c in w_copies:
                c.wait()
            for y in range(ny):
                wxb[y] = behind(wx[y], 1)

        once[f, 0] = oylo[f, 0]
        once[f, ny - 1] = oyhi[f, 0]
        for y in range(1, ny - 1):
            once[f, y, 0:1] = ozlo[f, y : y + 1]
            once[f, y, nz - 1 : nz] = ozhi[f, y : y + 1]

        def emit(y, c, t):
            t_ref[f, y] = c + t

        relax_slabs(lambda y: once[f, y], wx, wxb, wy, wz, emit)

    stream(nf, fetch, work, None)


def again_relax(p, wx, wy, wz, *faces):
    nf, ny, nz, nx = p.shape
    one = pltpu.VMEM((ny, nz, nx), jnp.float32)
    sem = pltpu.SemaphoreType.DMA
    return pl.pallas_call(
        again_kernel,
        in_specs=[FAR] * 4 + [NEAR] * 4,
        out_specs=NEAR,
        out_shape=jax.ShapeDtypeStruct(p.shape, jnp.float32),
        scratch_shapes=[pltpu.VMEM(p.shape, jnp.float32), one, one, one, one, sem((nf,)), sem((3,))],
        compiler_params=limit(32),
    )(far(p), far(wx), far(wy), far(wz), *faces)


def edge_kernel(
    t_ref, oylo, oyhi, ozlo, ozhi, yu, yd, zl, zr, lyu, lyd, lzl, lzr,
    r_far, g_ref, rbuf, high, low, r_sem,
):
    nf, ny, nz, nx = t_ref.shape

    def store(f):
        return pltpu.make_async_copy(rbuf.at[f], r_far.at[f], r_sem.at[f])

    def work(f):
        left = lzl[...] * (zl[f] - ozlo[f])
        right = lzr[...] * (zr[f] - ozhi[f])
        for y in range(ny):
            r = t_ref[f, y]
            if y == 0:
                r = r + lyu[...] * (yu[f, 0] - oylo[f, 0])
            if y == ny - 1:
                r = r + lyd[...] * (yd[f, 0] - oyhi[f, 0])
            r = add_first_row(r, left[y : y + 1])
            r = add_last_row(r, right[y : y + 1])
            rbuf[f, y] = r
            h = r.astype(jnp.bfloat16)
            at = pl.ds(pl.multiple_of(f * (ny * nz) + y * nz, nz), nz)
            high[at] = h
            low[at] = (r - h.astype(jnp.float32)).astype(jnp.bfloat16)

    stream(nf, None, work, store)

    def cross(a, b):
        return lax.dot_general(a, b, (((0,), (0,)), ((), ())), preferred_element_type=jnp.float32)

    half = nx // 2
    part = (slice(0, half), slice(half, nx))
    acc_hh, acc_hl = [], []
    for i in range(3):
        a, b = part[i // 2], part[(i + 1) // 2]
        acc_hh.append(cross(high[:, a], high[:, b]) + cross(low[:, a], low[:, b]))
    for i in range(4):
        acc_hl.append(cross(high[:, part[i // 2]], low[:, part[i % 2]]))
    per = half // BLK

    def inner_block(i, j):
        return slice(i % per * BLK, (i % per + 1) * BLK), slice(j % per * BLK, (j % per + 1) * BLK)

    t = 0
    for i in range(2 * per):
        for j in range(i, 2 * per):
            p, q = i // per, j // per
            a, b = inner_block(i, j)
            g_ref[t] = acc_hh[p + q][a, b] + acc_hl[2 * p + q][a, b] + acc_hl[2 * q + p][b, a].T
            t += 1

    drain(nf, store)


def edge_relax(t, faces, halos, links):
    nf, ny, nz, nx = t.shape
    cnt = nx // BLK
    nb = cnt * (cnt + 1) // 2
    return pl.pallas_call(
        edge_kernel,
        in_specs=[NEAR] * 13,
        out_specs=(FAR, NEAR),
        out_shape=(
            pltpu.HBM(t.shape, jnp.float32),
            jax.ShapeDtypeStruct((nb, BLK, BLK), jnp.float32),
        ),
        scratch_shapes=[pltpu.VMEM(t.shape, jnp.float32)]
        + [pltpu.VMEM((nf * ny * nz, nx), jnp.bfloat16)] * 2
        + [pltpu.SemaphoreType.DMA((nf,))],
        compiler_params=limit(32),
    )(t, *faces, *halos, *links)


def finish_kernel(g_ref, r_far, fac_ref, o_far, n_ref, panel, rbuf, obuf, high, low, r_sem, o_sem):
    count, chunk, width = rbuf.shape
    step = 256

    def fetch(i):
        return pltpu.make_async_copy(r_far.at[i], rbuf.at[i], r_sem.at[i])

    def store(i):
        return pltpu.make_async_copy(obuf.at[i], o_far.at[i], o_sem.at[i])

    for i in range(count):
        fetch(i).start()
    factor_kernel(g_ref, fac_ref, n_ref, panel)
    n = n_ref[...]
    h = n.astype(jnp.bfloat16)
    high[...] = h
    low[...] = (n - h.astype(jnp.float32)).astype(jnp.bfloat16)

    def project(i, carry):
        fetch(i).wait()
        r = rbuf[i]
        a = r.astype(jnp.bfloat16)
        b = (r - a.astype(jnp.float32)).astype(jnp.bfloat16)
        for lo in range(0, width, step):
            hi = lo + step

            def times(x, m):
                return lax.dot_general(
                    x[:, 0:hi], m[lo:hi, 0:hi], (((1,), (1,)), ((), ())), preferred_element_type=jnp.float32
                )

            obuf[i, :, lo:hi] = times(a, high) + (times(a, low) + times(b, high))
        store(i).start()
        return carry

    lax.fori_loop(0, count, project, 0)
    drain(count, store)


def factor_and_basis(blocks, rows, chunk=512):
    m, nx = rows.shape
    cut = (m // chunk, chunk, nx)
    big = pltpu.VMEM(cut, jnp.float32)
    sem = pltpu.SemaphoreType.DMA((m // chunk,))
    return pl.pallas_call(
        finish_kernel,
        in_specs=[NEAR, FAR],
        out_specs=(NEAR, FAR),
        out_shape=(jax.ShapeDtypeStruct((nx, nx), jnp.float32), pltpu.HBM(cut, jnp.float32)),
        scratch_shapes=[pltpu.VMEM((nx, nx), jnp.float32), pltpu.VMEM((BLK, 2 * BLK), jnp.float32), big, big]
        + [pltpu.VMEM((nx, nx), jnp.bfloat16)] * 2
        + [sem, sem],
        compiler_params=limit(32),
    )(blocks, far(rows.reshape(cut)))


BY = ("yh", "c")
BZ = ("x", "z", "yl")


def axis_count(axes):
    count = 1
    for axis in axes:
        count *= lax.axis_size(axis)
    return count


def from_next(piece, axes, step):
    n = axis_count(axes)
    return lax.ppermute(piece, axes, [(i + step, i) for i in range(n) if 0 <= i + step < n])


def on_device(fields, conductance):
    nfield, ny, nz, width = fields.shape

    def cells(ys, zs):
        return jnp.concatenate([fields[:, ys, zs], conductance[None, ys, zs]], axis=0)

    every = slice(None)
    ylo, yhi = cells(slice(0, 1), every), cells(slice(-1, None), every)
    zlo, zhi = cells(every, 0), cells(every, -1)

    def neighbours(ylo, yhi, zlo, zhi):
        return from_next(yhi, BY, -1), from_next(ylo, BY, 1), from_next(zhi, BZ, -1), from_next(zlo, BZ, 1)

    halo = neighbours(ylo, yhi, zlo, zhi)
    part, wx, wy, wz, *own = own_relax(fields, conductance)
    out = face_relax(*own, ylo, yhi, zlo, zhi, *halo)
    faces, links = out[:4], out[4:]
    halo = neighbours(*faces)
    twice = again_relax(part, wx, wy, wz, *faces)
    relaxed, blocks = edge_relax(twice, faces, halo, links)
    total_rows = nfield * ny * axis_count(BY) * nz * axis_count(BZ)
    blocks = sum_over_devices(blocks) / jnp.float32(total_rows)
    factor, basis = factor_and_basis(blocks, relaxed.reshape(-1, width))
    return (basis.reshape(relaxed.shape), factor)


def solution(mesh):
    fine = Mesh(mesh.devices.reshape(2, 2, 4, 4, 2), ("yh", "c", "x", "z", "yl"))
    return jax.shard_map(
        on_device,
        mesh=fine,
        in_specs=(P(None, BY, BZ, None), P(BY, BZ, None)),
        out_specs=(P(None, BY, BZ, None), P()),
        check_vma=False,
    )
```
